512 devices in a mesh: section: 8 (over x, core), blk: 32 (over z, y_hi), head: 2 (over y_lo).
Axes of the slice: x: 4, y: 8 (y_hi: 4, y_lo: 2; y = y_hi * 2 + y_lo), z: 8, core: 2. Of those that a mesh axis runs over, the one named last changes fastest.
Arguments:
- hidden_in: bfloat16 [4, 256, 1536], P(None, 'blk', 'head'), may hold values from -6 to 6
- w_qkv: bfloat16 [8, 1536, 3, 1536], P('section', 'blk', None, 'head'), may hold values from -0.15625 to 0.15625
- norm_gain: float32 [8, 1536], P('section'), may hold values from 0.5 to 1.5
- qk_gain: float32 [8, 2, 128], P('section'), may hold values from 1 to 2
- text_states: bfloat16 [8, 256, 1536], P('section'), may hold values from -6 to 6
- text_len: int32 [1], replicated, may hold values from 64 to 256
- patch_len: int32 [4], replicated, may hold values from 128 to 256
- stale_flags: int32 [4, 8], replicated, may hold values from 0 to 1, as said below
- stale_kv: bfloat16 [8, 2, 4, 256, 1536], P('section', None, None, 'blk', 'head'), may hold values from -6 to 6
Outputs:
- hidden_out: bfloat16 [8, 4, 256, 1536], P('section', None, 'blk', 'head')
- new_cache: bfloat16 [8, 2, 4, 256, 1536], P('section', None, None, 'blk', 'head')
The draws below stay inside these ranges and needn't reach their ends.
Inputs may be any that keep to these rules, and one draw needn't show every extreme that they name: `stale_flags`: 1 means that the micro-batch uses the previous step's keys and values at that layer, 0 that it uses its fresh ones; every layer has at least one micro-batch flagged 1 and at least one flagged 0.
All inputs are finite; a program needn't handle non-finite values.
Results may differ from the reference program's by a relative error of at most 0.02.
Values may be sent and summed in bfloat16 or wider, within the bound.
No kernel may reach another device: no remote copies, remote signals or barrier semaphores. Data moves between devices by JAX's collectives and lax.ppermute only.
A program may use at most 64 MiB of HBM per device.

```python
import math
import jax
import jax.numpy as jnp
from jax import lax

D = 1536
HEADS = 12
HEAD_DIM = 128
TEXT = 256
MICRO = 4
LAYERS = 8
PATCH = 256


def draw_stale_flags(key, part):
    bits_key = jax.random.fold_in(key, 101)
    pick_key = jax.random.fold_in(key, 202)
    random_bits = jax.random.randint(bits_key, (MICRO, LAYERS), 0, 2).astype(jnp.int32)
    chosen = jax.random.randint(pick_key, (1, LAYERS), 0, MICRO).astype(jnp.int32)
    rows = jnp.arange(MICRO, dtype=jnp.int32)[:, None]
    forced_on = rows == chosen
    forced_off = rows == (chosen + 1) % MICRO
    flags = jnp.where(forced_on, 1, jnp.where(forced_off, 0, random_bits))
    return flags.astype(jnp.int32)


def plant(array, own_key, low, high):
    spot = [jax.random.randint(jax.random.fold_in(own_key, axis), (), 0, length) for axis, length in enumerate(array.shape)]
    main_axis = array.shape.index(max(array.shape))
    next_to = spot[:main_axis] + [(spot[main_axis] + 1) % array.shape[main_axis]] + spot[main_axis + 1:]
    return array.at[tuple(spot)].set(low).at[tuple(next_to)].set(high)


def levels(rng, extent, pieces, smallest, top_value):
    def one(dim, parts):
        steps = jax.random.uniform(jax.random.fold_in(jax.random.fold_in(rng, 6), dim), (parts,), jnp.float32, smallest / len(pieces), top_value / len(pieces))
        return jnp.repeat(jnp.exp(steps), extent[dim] // parts).reshape((-1,) + (1,) * (len(extent) - dim - 1))

    loudness = one(*pieces[0])
    for cut in pieces[1:]:
        loudness = loudness * one(*cut)
    return loudness


def gaussian(own_key, dims, scale, reach, split=(), kind=jnp.bfloat16):
    result = jax.random.normal(own_key, dims, jnp.float32) * scale
    if len(split) > 0:
        result = levels(own_key, dims, split, -0.22, 0.18) * result
    return jnp.clip(result, min=-reach, max=reach).astype(kind)


def setup_inputs(seed: int = 0) -> dict:
    splits = jax.random.split(jax.random.key(seed), 10)
    hidden_in = gaussian(splits[0], (MICRO, PATCH, D), 1.0, 6.0, ((1, 32), (2, 2)))
    w_qkv = gaussian(splits[1], (LAYERS, D, 3, HEADS * HEAD_DIM), D ** -0.5, 0.15625, ((0, 8), (1, 32), (3, 2)))
    norm_gain = jnp.clip(1.0 + 0.1 * jax.random.normal(splits[2], (LAYERS, D), jnp.float32), 0.5, 1.5)
    qk_gain = jnp.clip(jnp.exp(math.log(2.0) - 0.6931472 * jax.random.uniform(splits[3], (LAYERS, 2, HEAD_DIM), jnp.float32) ** levels(splits[3], (LAYERS, 2, HEAD_DIM), ((0, 8),), -0.2, 0.2)), 1.0, 2.0)
    text_states = gaussian(splits[4], (LAYERS, TEXT, D), 1.0, 6.0, ((0, 8),))
    text_len = jax.random.randint(splits[5], (1,), TEXT // 4, TEXT + 1).astype(jnp.int32)
    patch_len = plant(jax.random.randint(splits[6], (MICRO,), PATCH // 2, PATCH + 1), jax.random.fold_in(splits[6], 1), PATCH // 2, PATCH).astype(jnp.int32)
    stale_flags = draw_stale_flags(jax.random.fold_in(splits[9], 71), 0)
    stale_kv = gaussian(splits[8], (LAYERS, 2, MICRO, PATCH, HEADS * HEAD_DIM), 1.0, 6.0, ((0, 8), (3, 32), (4, 2)))
    return dict(hidden_in=hidden_in, w_qkv=w_qkv, norm_gain=norm_gain, qk_gain=qk_gain, text_states=text_states, text_len=text_len, patch_len=patch_len, stale_flags=stale_flags, stale_kv=stale_kv)


def norm_rows(values, row_gain):
    return values * lax.rsqrt(lax.optimization_barrier(jnp.mean(values * values, axis=-1, keepdims=True)) + 1e-06) * row_gain

def attend_part(queries, key_rows, value_rows, key_mask):
    scores = jnp.einsum('qhd,khd->hqk', queries.astype(jnp.float32), key_rows.astype(jnp.float32), precision=lax.Precision.HIGHEST) * HEAD_DIM ** (-0.5)
    probs = jnp.where(key_mask[None, None, :], jnp.exp(scores), 0.0)
    numerator = jnp.einsum('hqk,khd->qhd', probs.astype(jnp.bfloat16).astype(jnp.float32), value_rows.astype(jnp.float32), precision=lax.Precision.HIGHEST)
    return (numerator, lax.optimization_barrier(jnp.sum(probs, axis=2)))

def reference(hidden_in, w_qkv, norm_gain, qk_gain, text_states, text_len, patch_len, stale_flags, stale_kv):
    width = HEADS * HEAD_DIM
    text_mask = jnp.arange(TEXT) < text_len[0]
    positions = jnp.arange(PATCH)
    state_all = hidden_in
    hidden_layers = []
    cache_layers = []
    for layer_idx in range(LAYERS):
        weight_flat = w_qkv[layer_idx].reshape(D, 3 * width)
        row_gain = norm_gain[layer_idx]
        query_gain = qk_gain[layer_idx, 0]
        key_gain = qk_gain[layer_idx, 1]
        text_normed = norm_rows(text_states[layer_idx].astype(jnp.float32), row_gain).astype(jnp.bfloat16)
        text_kv = jnp.dot(text_normed, weight_flat[:, width:], preferred_element_type=jnp.float32).astype(jnp.bfloat16)
        text_kv = text_kv.reshape(TEXT, 2, HEADS, HEAD_DIM)
        text_keys = norm_rows(text_kv[:, 0].astype(jnp.float32), key_gain).astype(jnp.bfloat16)
        text_values = text_kv[:, 1]
        layer_hidden = []
        layer_cache = []
        for micro_idx in range(MICRO):
            rows_in = state_all[micro_idx]
            normed = norm_rows(rows_in.astype(jnp.float32), row_gain).astype(jnp.bfloat16)
            projected = jnp.dot(normed, weight_flat, preferred_element_type=jnp.float32).reshape(PATCH, 3, width)
            fresh_kv = jnp.moveaxis(projected[:, 1:], 1, 0).astype(jnp.bfloat16)
            kept_kv = jnp.where(stale_flags[micro_idx, layer_idx] == 1, stale_kv[layer_idx, :, micro_idx], fresh_kv)
            key_rows = norm_rows(kept_kv[0].astype(jnp.float32).reshape(PATCH, HEADS, HEAD_DIM), key_gain).astype(jnp.bfloat16)
            value_rows = kept_kv[1].reshape(PATCH, HEADS, HEAD_DIM)
            queries = norm_rows(projected[:, 0].reshape(PATCH, HEADS, HEAD_DIM), query_gain).astype(jnp.bfloat16)
            text_num, text_den = attend_part(queries, text_keys, text_values, text_mask)
            own_num, own_den = attend_part(queries, key_rows, value_rows, positions < patch_len[micro_idx])
            attended = (text_num + own_num) / jnp.transpose(text_den + own_den)[:, :, None]
            layer_hidden.append((rows_in.astype(jnp.float32) + attended.reshape(PATCH, width)).astype(jnp.bfloat16))
            layer_cache.append(fresh_kv)
        state_all = jnp.stack(layer_hidden)
        hidden_layers.append(state_all)
        cache_layers.append(jnp.stack(layer_cache, axis=1))
    return (jnp.stack(hidden_layers), jnp.stack(cache_layers))
```

```python
import functools
import jax
import jax.numpy as jnp
from jax import lax
from jax.experimental import pallas as pl
from jax.experimental.pallas import tpu as pltpu
from jax.sharding import PartitionSpec as P

AX = ("section", "blk", "head")
PLANE = ("blk", "head")
BF = jnp.bfloat16
F32 = jnp.float32
ROWS = 48
QUAD = [(a, c) for a in range(2) for c in range(2)]
TARGET = {(half, side): (1 + side, 2 - half) for half in range(2) for side in range(2)}


def place(z, y):
    return (z % 8) * 8 + y % 8


def quadrant_groups():
    return [[place(z + 4 * a, y + 4 * c) for a, c in QUAD] for z in range(4) for y in range(4)]


def block_groups():
    order = [TARGET[half, side] for half in range(2) for side in range(2)]
    return [[place(z + 2 * i, y + 2 * j) for z, y in order] for i in range(4) for j in range(4)]


def weight_pairs(zl, swapped, sections):
    pairs = []
    for s in range(sections):
        for a, c in QUAD:
            for half in range(2):
                for yh in range(2):
                    z, y = TARGET[half, 1 - yh if swapped else yh]
                    pairs.append((
                        s * 64 + place(4 * a + zl, 4 * c + 2 * yh + half),
                        s * 64 + place(4 * a + z, 4 * c + y),
                    ))
    return pairs


def hop_pairs(step):
    return [
        (step * 64 + place(4 * a + z, 4 * c + y), (step + 1) * 64 + place(4 * a + z, 4 * c + y))
        for a, c in QUAD
        for z, y in TARGET.values()
    ]


def head_norm(block, gain):
    mean = jnp.mean(block * block, axis=-1, keepdims=True)
    return block * lax.rsqrt(mean + 1e-06) * gain


def prep_kernel(
    heads, scalars, *refs
):
    pieces, (text_ref, gain_ref, qk_ref, stale_ref), (w_ref, tk_ref, tv_ref, sk_ref), (sems,) = (
        refs[:8], refs[8:12], refs[12:16], refs[16:]
    )
    width = heads * 128
    side = scalars[0]
    copies = []
    for zl in range(4):
        for swapped in range(2):
            yh = side if swapped == 0 else 1 - side
            for k, (a, c) in enumerate(QUAD):
                block = (4 * a + zl) * 4 + 2 * c + yh
                row = pl.multiple_of(block * ROWS, 16)
                for part in range(3):
                    copy = pltpu.make_async_copy(
                        pieces[2 * zl + swapped].at[k, pl.ds(part * ROWS, ROWS), :],
                        w_ref.at[pl.ds(row, ROWS), pl.ds(part * width, width)],
                        sems.at[len(copies)],
                    )
                    copy.start()
                    copies.append(copy)
    text = text_ref[...].astype(F32)
    mean = jnp.mean(text * text, axis=-1, keepdims=True)
    normed = (text * lax.rsqrt(mean + 1e-06) * gain_ref[...]).astype(BF)
    key_gain = qk_ref[1:2, :]
    for h in range(heads):
        cols = slice(h * 128, (h + 1) * 128)
        sk_ref[:, cols] = head_norm(stale_ref[0, :, cols].astype(F32), key_gain).astype(BF)
    for copy in copies:
        copy.wait()
    kv = jnp.dot(normed, w_ref[:, width:], preferred_element_type=F32).astype(BF)
    for h in range(heads):
        cols = slice(h * 128, (h + 1) * 128)
        tk_ref[:, cols] = head_norm(kv[:, cols].astype(F32), key_gain).astype(BF)
    tv_ref[...] = kv[:, width:]


def layer_kernel(
    heads, scalars, x_ref, own_ref, w_ref, gain_ref, qk_ref, tk_ref, tv_ref, sk_ref, sv_ref,
    out_ref, cache_ref,
):
    width = heads * 128
    stale, limit, text_limit = scalars[1] == 1, scalars[2], scalars[3]
    parts = [x_ref[q].astype(F32) for q in range(4)]
    total = sum(jnp.sum(part * part, axis=-1, keepdims=True) for part in parts)
    scale = lax.rsqrt(total / (4 * width) + 1e-06)
    normed = jnp.concatenate(
        [
            (part * scale * gain_ref[:, q * width : (q + 1) * width]).astype(BF)
            for q, part in enumerate(parts)
        ],
        axis=1,
    )
    projected = jnp.dot(normed, w_ref[...], preferred_element_type=F32)
    fresh = projected[:, width:].astype(BF)
    cache_ref[0] = fresh[:, :width]
    cache_ref[1] = fresh[:, width:]
    query_gain, key_gain = qk_ref[0:1, :], qk_ref[1:2, :]
    tokens = out_ref.shape[0]
    own_mask = lax.broadcasted_iota(jnp.int32, (tokens, tokens), 1) < limit
    text_mask = lax.broadcasted_iota(jnp.int32, (tokens, tk_ref.shape[0]), 1) < text_limit
    contract = (((1,), (1,)), ((), ()))
    for h in range(heads):
        cols = slice(h * 128, (h + 1) * 128)
        queries = head_norm(projected[:, cols], query_gain).astype(BF)
        keys = head_norm(fresh[:, cols].astype(F32), key_gain).astype(BF)
        keys = jnp.where(stale, sk_ref[:, cols], keys)
        values = jnp.where(stale, sv_ref[:, cols], fresh[:, width + h * 128 : width + (h + 1) * 128])
        own = lax.dot_general(queries, keys, contract, preferred_element_type=F32)
        own = jnp.where(own_mask, jnp.exp(own * 128 ** (-0.5)), 0.0)
        text = lax.dot_general(queries, tk_ref[:, cols], contract, preferred_element_type=F32)
        text = jnp.where(text_mask, jnp.exp(text * 128 ** (-0.5)), 0.0)
        numerator = jnp.dot(text.astype(BF), tv_ref[:, cols], preferred_element_type=F32)
        numerator += jnp.dot(own.astype(BF), values, preferred_element_type=F32)
        denominator = jnp.sum(own, axis=1, keepdims=True) + jnp.sum(text, axis=1, keepdims=True)
        out_ref[:, cols] = (own_ref[:, cols].astype(F32) + numerator / denominator).astype(BF)


def shards(
    hidden_in, w_qkv, norm_gain, qk_gain, text_states, text_len, patch_len, stale_flags, stale_kv
):
    sections = lax.axis_size("section")
    section = lax.axis_index("section")
    blk = lax.axis_index("blk")
    half = lax.axis_index("head")
    micros, tok, half_width = hidden_in.shape
    width = half_width // 2
    heads = width // 128
    z, y_hi = blk // 4, blk % 4
    micro = 2 * (z // 4) + y_hi // 2
    side = jnp.where(z % 4 == 2, 1, 0)
    swap = y_hi % 2 == 1

    w = jnp.moveaxis(w_qkv[0], 1, 0).reshape(3, ROWS, 2, width)
    w = jnp.moveaxis(w, 2, 0).reshape(1, 2, 3 * ROWS, width)
    old = jnp.moveaxis(stale_kv[0].reshape(2, micros, tok, 2, width), (1, 3), (0, 1))
    first = jnp.moveaxis(hidden_in.reshape(micros, tok, 2, width), 2, 1)
    packed = jnp.concatenate(
        [
            jnp.broadcast_to(w, (micros,) + w.shape[1:]),
            old.reshape(micros, 2, 2 * tok, width),
            first,
        ],
        axis=2,
    )
    packed = jnp.where(swap, packed[:, ::-1], packed)
    spread = lax.all_to_all(
        packed, PLANE, 0, 0, axis_index_groups=quadrant_groups(), tiled=True
    )
    lanes = (spread[:, 0], spread[:, 1])
    pieces = [
        lax.ppermute(lanes[swapped], AX, weight_pairs(zl, swapped, sections))
        for zl in range(4)
        for swapped in range(2)
    ]
    tails = [piece[:, 3 * ROWS :] for piece in pieces]
    straight = jnp.stack([jnp.stack(tails[2 * i : 2 * i + 2]) for i in range(4)])
    straight = jnp.where(side == 1, straight[:, ::-1], straight)
    tail = straight.reshape(4, 2, 2, 2, 3, tok, width).transpose(4, 2, 0, 3, 1, 5, 6)
    tail = tail.reshape(3, 32 * tok, width)
    stale_value, state = tail[1], tail[2]

    flag = lax.dynamic_slice(stale_flags, (micro, section), (1, 1))[0, 0]
    limit = lax.dynamic_slice(patch_len, (micro,), (1,))[0]
    scalars = jnp.stack([side, flag, limit, text_len[0]]).astype(jnp.int32)
    tokens, text_count, depth = 32 * tok, text_states.shape[1], text_states.shape[2]
    vmem = pl.BlockSpec(memory_space=pltpu.VMEM)
    smem = pl.BlockSpec(memory_space=pltpu.SMEM)
    qk = qk_gain[0]
    block = jax.ShapeDtypeStruct((tokens, width), BF)
    weights, text_key, text_value, stale_key = pl.pallas_call(
        functools.partial(prep_kernel, heads),
        out_shape=[jax.ShapeDtypeStruct((depth, 3 * width), BF)]
        + [jax.ShapeDtypeStruct((text_count, width), BF)] * 2
        + [block],
        in_specs=[smem] + [pl.BlockSpec(memory_space=pl.ANY)] * 8 + [vmem] * 4,
        out_specs=[vmem] * 4,
        scratch_shapes=[pltpu.SemaphoreType.DMA((96,))],
        compiler_params=pltpu.CompilerParams(vmem_limit_bytes=40 * 2**20),
        name="prepare",
    )(scalars, *pieces, text_states[0], norm_gain, qk, tail)

    layer = pl.pallas_call(
        functools.partial(layer_kernel, heads),
        out_shape=[block, jax.ShapeDtypeStruct((2, tokens, width), BF)],
        in_specs=[smem] + [vmem] * 9,
        out_specs=[vmem] * 2,
        compiler_params=pltpu.CompilerParams(vmem_limit_bytes=40 * 2**20),
        name="layer",
    )
    kept_hidden = kept_cache = None
    for step in range(sections):
        if step:
            state = lax.ppermute(state, AX, hop_pairs(step - 1))
        whole = lax.all_to_all(
            jnp.broadcast_to(state[None], (4,) + state.shape),
            PLANE, 0, 0, axis_index_groups=block_groups(), tiled=True,
        )
        state, cache = layer(
            scalars, whole, state, weights, norm_gain, qk, text_key, text_value, stale_key,
            stale_value,
        )
        if step:
            here = section == step
            kept_hidden = jnp.where(here, state, kept_hidden)
            kept_cache = jnp.where(here, cache, kept_cache)
        else:
            kept_hidden, kept_cache = state, cache

    result = jnp.concatenate([kept_hidden[None], kept_cache]).reshape(3, 32, tok, width)
    result = lax.all_to_all(jnp.moveaxis(result, 1, 0), "blk", 0, 0, tiled=True)
    chosen = []
    for a, c in QUAD:
        for which in range(2):
            options = []
            for h in range(2):
                tz, ty = TARGET[h, which]
                options.append(result[(4 * a + tz) * 4 + 2 * c + ty // 2])
            chosen.append(jnp.where(half == 1, options[1], options[0]))
    out = jnp.stack(chosen).reshape(micros, 2, 3, tok, width).transpose(2, 0, 3, 1, 4)
    out = out.reshape(3, micros, tok, half_width)
    return (out[0][None], out[1:][None])


def solution(mesh):
    in_specs = (
        P(None, "blk", "head"),
        P("section", "blk", None, "head"),
        P("section", None),
        P("section", None, None),
        P("section", None, None),
        P(),
        P(),
        P(),
        P("section", None, None, "blk", "head"),
    )
    out_specs = (P("section", None, "blk", "head"), P("section", None, None, "blk", "head"))
    return jax.shard_map(shards, mesh=mesh, in_specs=in_specs, out_specs=out_specs, check_vma=False)
```

```python
import functools
import jax
import jax.numpy as jnp
from jax import lax
from jax.experimental import pallas as pl
from jax.experimental.pallas import tpu as pltpu
from jax.sharding import PartitionSpec as P

AX = ("section", "blk", "head")
PLANE = ("blk", "head")
BF = jnp.bfloat16
F32 = jnp.float32
ROWS = 48
TAIL = 32
PIECE = 3 * ROWS + TAIL
HBM = pl.BlockSpec(memory_space=pltpu.HBM)
VMEM = pl.BlockSpec(memory_space=pltpu.VMEM)
SMEM = pl.BlockSpec(memory_space=pltpu.SMEM)


def at(section, z, y):
    return section * 64 + z * 8 + y


def ring_groups(sections):
    groups = []
    for s in range(sections):
        for i in range(8):
            groups.append([at(s, j, i) if s % 2 == 0 else at(s, i, j) for j in range(8)])
    return groups


def even_pairs(k, sections):
    return [
        (at(s, z, 2 * k + half), at(s, z, z // 2 * 2 + half))
        for s in range(0, sections, 2)
        for z in range(8)
        for half in range(2)
    ]


def odd_pairs(i, lane, sections):
    return [
        (at(s, 2 * i + low, y), at(s, y // 2 * 2 + (low ^ lane), y))
        for s in range(1, sections, 2)
        for low in range(2)
        for y in range(8)
    ]


def block_groups(odd):
    order = [(h, q) if odd else (q, h) for h in range(2) for q in range(2)]
    return [[at(0, 2 * i + z, 2 * j + y) for z, y in order] for i in range(4) for j in range(4)]


def hop_pairs(step):
    return [
        (at(step, 2 * m + i, 2 * m + j), at(step + 1, 2 * m + i, 2 * m + j))
        for m in range(4)
        for i in range(2)
        for j in range(2)
    ]


def position():
    section, blk, head = lax.axis_index("section"), lax.axis_index("blk"), lax.axis_index("head")
    z_low = lax.rem(blk // 4, 2)
    odd = lax.rem(section, 2)
    half = jnp.where(odd == 1, z_low, head)
    side = jnp.where(odd == 1, head, z_low)
    return section, odd, blk // 8, half, side


def head_norm(block, gain):
    mean = jnp.mean(block * block, axis=-1, keepdims=True)
    return block * lax.rsqrt(mean + 1e-06) * gain


def prep_kernel(heads, *refs):
    evens, odds, (text_ref, gain_ref, qk_ref) = refs[:4], refs[4:12], refs[12:15]
    w_ref, tk_ref, tv_ref, sk_ref, sv_ref, state_ref = refs[15:21]
    tails, stale_key, stale_value, state, sems = refs[21:]
    width = heads * 128
    _, odd, _, half, _ = position()

    def block_copies(source, block, first):
        row = block * ROWS
        if not isinstance(row, int):
            row = pl.multiple_of(row, 16)
        made = [
            pltpu.make_async_copy(
                source.at[pl.ds(part * ROWS, ROWS), :],
                w_ref.at[pl.ds(row, ROWS), pl.ds(part * width, width)],
                sems.at[first + part],
            )
            for part in range(3)
        ]
        made.append(
            pltpu.make_async_copy(
                source.at[pl.ds(3 * ROWS, TAIL), :], tails.at[block], sems.at[first + 3]
            )
        )
        return made

    even_copies = []
    for k in range(4):
        for z in range(8):
            even_copies += block_copies(evens[k].at[z], z * 4 + k, len(even_copies))
    odd_copies = []
    for i in range(4):
        for lane in range(2):
            z = 2 * i + (half if lane == 0 else 1 - half)
            for y_hi in range(4):
                odd_copies += block_copies(
                    odds[2 * i + lane].at[y_hi], z * 4 + y_hi, len(odd_copies)
                )

    @pl.when(odd == 0)
    def _():
        for copy in even_copies:
            copy.start()

    @pl.when(odd == 1)
    def _():
        for copy in odd_copies:
            copy.start()

    text = text_ref[...].astype(F32)
    mean = jnp.mean(text * text, axis=-1, keepdims=True)
    normed = (text * lax.rsqrt(mean + 1e-06) * gain_ref[...]).astype(BF)
    key_gain = qk_ref[1:2, :]

    @pl.when(odd == 0)
    def _():
        for copy in even_copies:
            copy.wait()

    @pl.when(odd == 1)
    def _():
        for copy in odd_copies:
            copy.wait()

    for b in range(32):
        tail = tails[b].astype(F32)
        stale_key[8 * b : 8 * b + 8, :] = tail[0:8]
        stale_value[8 * b : 8 * b + 8, :] = tail[8:16]
        state[8 * b : 8 * b + 8, :] = tail[16:24]
    sv_ref[...] = stale_value[...].astype(BF)
    state_ref[...] = state[...].astype(BF)
    kv = jnp.dot(normed, w_ref[:, width:], preferred_element_type=F32).astype(BF)
    for h in range(heads):
        cols = slice(h * 128, (h + 1) * 128)
        sk_ref[:, cols] = head_norm(stale_key[:, cols], key_gain).astype(BF)
        tk_ref[:, cols] = head_norm(kv[:, cols].astype(F32), key_gain).astype(BF)
    tv_ref[...] = kv[:, width:]


def layer_kernel(
    heads, flag_ref, patch_ref, text_len_ref, x_ref, w_ref, gain_ref, qk_ref, tk_ref, tv_ref,
    sk_ref, sv_ref, out_ref, cache_ref,
):
    width = heads * 128
    section, _, micro, half, side = position()
    stale, limit, text_limit = flag_ref[micro, section] == 1, patch_ref[micro], text_len_ref[0]
    own_ref = x_ref.at[2 * half + side]
    parts = [x_ref[q].astype(F32) for q in range(4)]
    total = sum(jnp.sum(part * part, axis=-1, keepdims=True) for part in parts)
    scale = lax.rsqrt(total / (4 * width) + 1e-06)
    normed = jnp.concatenate(
        [
            (part * scale * gain_ref[:, q * width : (q + 1) * width]).astype(BF)
            for q, part in enumerate(parts)
        ],
        axis=1,
    )
    projected = jnp.dot(normed, w_ref[...], preferred_element_type=F32)
    fresh = projected[:, width:].astype(BF)
    cache_ref[0] = fresh[:, :width]
    cache_ref[1] = fresh[:, width:]
    query_gain, key_gain = qk_ref[0:1, :], qk_ref[1:2, :]
    tokens = out_ref.shape[0]
    own_mask = lax.broadcasted_iota(jnp.int32, (tokens, tokens), 1) < limit
    text_mask = lax.broadcasted_iota(jnp.int32, (tokens, tk_ref.shape[0]), 1) < text_limit
    contract = (((1,), (1,)), ((), ()))
    for h in range(heads):
        cols = slice(h * 128, (h + 1) * 128)
        queries = head_norm(projected[:, cols], query_gain).astype(BF)
        keys = head_norm(fresh[:, cols].astype(F32), key_gain).astype(BF)
        keys = jnp.where(stale, sk_ref[:, cols], keys)
        values = jnp.where(stale, sv_ref[:, cols], fresh[:, width + h * 128 : width + (h + 1) * 128])
        own = lax.dot_general(queries, keys, contract, preferred_element_type=F32)
        own = jnp.where(own_mask, jnp.exp(own * 128 ** (-0.5)), 0.0)
        text = lax.dot_general(queries, tk_ref[:, cols], contract, preferred_element_type=F32)
        text = jnp.where(text_mask, jnp.exp(text * 128 ** (-0.5)), 0.0)
        numerator = jnp.dot(text.astype(BF), tv_ref[:, cols], preferred_element_type=F32)
        numerator += jnp.dot(own.astype(BF), values, preferred_element_type=F32)
        denominator = jnp.sum(own, axis=1, keepdims=True) + jnp.sum(text, axis=1, keepdims=True)
        out_ref[:, cols] = (own_ref[:, cols].astype(F32) + numerator / denominator).astype(BF)


def shards(
    hidden_in, w_qkv, norm_gain, qk_gain, text_states, text_len, patch_len, stale_flags, stale_kv
):
    sections = lax.axis_size("section")
    section = lax.axis_index("section")
    z = lax.axis_index("blk") // 4
    head = lax.axis_index("head")
    odd = section % 2 == 1
    micros, tok, half_width = hidden_in.shape
    width = half_width // 2
    heads = width // 128
    tokens, text_count, depth = 32 * tok, text_states.shape[1], text_states.shape[2]

    w = jnp.moveaxis(w_qkv[0], 1, 0).reshape(3, ROWS, 2, width)
    w = jnp.moveaxis(w, 2, 0).reshape(1, 2, 3 * ROWS, width)
    old = jnp.moveaxis(stale_kv[0].reshape(2, micros, tok, 2, width), (1, 3), (0, 1))
    first = jnp.moveaxis(hidden_in.reshape(micros, tok, 2, width), 2, 1)
    packed = jnp.concatenate(
        [
            jnp.broadcast_to(w, (micros,) + w.shape[1:]),
            old.reshape(micros, 2, 2 * tok, width),
            first,
            jnp.zeros((micros, 2, TAIL - 3 * tok, width), BF),
        ],
        axis=2,
    ).reshape(2 * micros, PIECE, width)
    ring = lax.all_to_all(packed, AX, 0, 0, axis_index_groups=ring_groups(sections), tiled=True)
    evens = [lax.ppermute(ring, AX, even_pairs(k, sections)) for k in range(4)]
    by_half = ring.reshape(4, 2, PIECE, width)
    low = z % 2 == 1
    lanes = (
        jnp.where(low, by_half[:, 1], by_half[:, 0]),
        jnp.where(low, by_half[:, 0], by_half[:, 1]),
    )
    odds = [
        lax.ppermute(lanes[lane], AX, odd_pairs(i, lane, sections))
        for i in range(4)
        for lane in range(2)
    ]

    qk = qk_gain[0]
    block = jax.ShapeDtypeStruct((tokens, width), BF)
    text_block = jax.ShapeDtypeStruct((text_count, width), BF)
    weights, text_key, text_value, stale_key, stale_value, state = pl.pallas_call(
        functools.partial(prep_kernel, heads),
        out_shape=[jax.ShapeDtypeStruct((depth, 3 * width), BF), text_block, text_block]
        + [block] * 3,
        in_specs=[HBM] * 12 + [VMEM] * 3,
        out_specs=[VMEM] * 6,
        scratch_shapes=[
            pltpu.VMEM((32, TAIL, width), BF),
            pltpu.VMEM((tokens, width), F32),
            pltpu.VMEM((tokens, width), F32),
            pltpu.VMEM((tokens, width), F32),
            pltpu.SemaphoreType.DMA((128,)),
        ],
        compiler_params=pltpu.CompilerParams(vmem_limit_bytes=40 * 2**20),
        name="prepare",
    )(*evens, *odds, text_states[0], norm_gain, qk)

    layer = pl.pallas_call(
        functools.partial(layer_kernel, heads),
        out_shape=[block, jax.ShapeDtypeStruct((2, tokens, width), BF)],
        in_specs=[SMEM] * 3 + [VMEM] * 8,
        out_specs=[VMEM] * 2,
        compiler_params=pltpu.CompilerParams(vmem_limit_bytes=40 * 2**20),
        name="layer",
    )

    def advance(step, entering):
        whole = lax.all_to_all(
            jnp.broadcast_to(entering[None], (4,) + entering.shape),
            PLANE, 0, 0,
            axis_index_groups=block_groups(step > 0 and step % 2 == 0),
            tiled=True,
        )
        return layer(
            stale_flags, patch_len, text_len, whole, weights, norm_gain, qk, text_key, text_value,
            stale_key, stale_value,
        )

    kept = (state, jnp.zeros((2, tokens, width), BF))
    for step in range(sections):
        entering = lax.ppermute(kept[0], AX, hop_pairs(step - 1)) if step else state
        kept = lax.cond(
            section == step,
            lambda entering, *kept: tuple(advance(step, entering)),
            lambda entering, *kept: tuple(kept),
            entering, *kept,
        )

    result = jnp.concatenate([kept[0][None], kept[1]]).reshape(3, 32, tok, width)
    result = lax.all_to_all(jnp.moveaxis(result, 1, 0), "blk", 0, 0, tiled=True)
    found = [
        jnp.stack([result[(2 * m + j) * 4 + m] for m in range(micros)]) for j in range(2)
    ]
    swap = [
        (at(s, 0, 0) + 2 * b + h, at(s, 0, 0) + 2 * b + 1 - h)
        for s in range(1, sections, 2)
        for b in range(32)
        for h in range(2)
    ]
    other = lax.ppermute(jnp.where(head == 0, found[1], found[0]), AX, swap)
    left = jnp.where(odd & (head == 1), other, found[0])
    right = jnp.where(odd & (head == 0), other, found[1])
    out = jnp.stack([left, right]).transpose(2, 1, 3, 0, 4)
    out = out.reshape(3, micros, tok, half_width)
    return (out[0][None], out[1:][None])


def solution(mesh):
    in_specs = (
        P(None, "blk", "head"),
        P("section", "blk", None, "head"),
        P("section", None),
        P("section", None, None),
        P("section", None, None),
        P(),
        P(),
        P(),
        P("section", None, None, "blk", "head"),
    )
    out_specs = (P("section", None, "blk", "head"), P("section", None, None, "blk", "head"))
    return jax.shard_map(shards, mesh=mesh, in_specs=in_specs, out_specs=out_specs, check_vma=False)
```

```python
import functools
import jax
import jax.numpy as jnp
from jax import lax
from jax.experimental import pallas as pl
from jax.experimental.pallas import tpu as pltpu
from jax.sharding import PartitionSpec as P

AX = ("section", "blk", "head")
PLANE = ("blk", "head")
BF = jnp.bfloat16
F32 = jnp.float32
ROWS = 48
TAIL = 32
PIECE = 3 * ROWS + TAIL
MOVES = [(2, 0), (2, 1), (1, 0), (1, 1), (3, 0), (3, 1), (0, 1)]
HBM = pl.BlockSpec(memory_space=pltpu.HBM)
VMEM = pl.BlockSpec(memory_space=pltpu.VMEM)
SMEM = pl.BlockSpec(memory_space=pltpu.SMEM)


def at(section, z, y):
    return section * 64 + z * 8 + y


def ring_groups(sections):
    groups = []
    for s in range(sections):
        for i in range(8):
            groups.append([at(s, j, i) if s % 2 == 0 else at(s, i, j) for j in range(8)])
    return groups


def move_pairs(ahead, lane, sections):
    even = [
        (at(s, z, (2 * (z // 2 + ahead)) % 8 + half), at(s, z, z // 2 * 2 + half))
        for s in range(0, sections, 2)
        for z in range(8)
        for half in range(2)
    ]
    odd = [
        (at(s, (2 * (y // 2 + ahead)) % 8 + low, y), at(s, y // 2 * 2 + (low ^ lane), y))
        for s in range(1, sections, 2)
        for low in range(2)
        for y in range(8)
    ]
    return odd if ahead == 0 else even + odd


def block_groups(odd):
    order = [(h, q) if odd else (q, h) for h in range(2) for q in range(2)]
    return [[at(0, 2 * i + z, 2 * j + y) for z, y in order] for i in range(4) for j in range(4)]


def hop_pairs(step):
    return [
        (at(step, 2 * m + i, 2 * m + j), at(step + 1, 2 * m + i, 2 * m + j))
        for m in range(4)
        for i in range(2)
        for j in range(2)
    ]


def position():
    section, blk, head = lax.axis_index("section"), lax.axis_index("blk"), lax.axis_index("head")
    z_low = lax.rem(blk // 4, 2)
    odd = lax.rem(section, 2)
    half = jnp.where(odd == 1, z_low, head)
    side = jnp.where(odd == 1, head, z_low)
    return section, odd, blk // 8, half, side


def head_norm(block, gain):
    mean = jnp.mean(block * block, axis=-1, keepdims=True)
    return block * lax.rsqrt(mean + 1e-06) * gain


def prep_kernel(heads, *refs):
    pieces, (text_ref, gain_ref, qk_ref), w_ref = refs[:9], refs[9:12], refs[12]
    tk_ref, tv_ref, sk_ref, sv_ref, state_ref = refs[13:18]
    tails, stale_key, stale_value, state, sems = refs[18:]
    width = heads * 128
    _, odd, micro, half, _ = position()

    def block_copies(source, block, first):
        row = pl.multiple_of(block * ROWS, 16)
        made = [
            pltpu.make_async_copy(
                source.at[pl.ds(part * ROWS, ROWS), :],
                w_ref.at[pl.ds(row, ROWS), pl.ds(part * width, width)],
                sems.at[first + part],
            )
            for part in range(3)
        ]
        made.append(
            pltpu.make_async_copy(
                source.at[pl.ds(3 * ROWS, TAIL), :], tails.at[block], sems.at[first + 3]
            )
        )
        return made

    even_copies, odd_copies = [], []
    for ahead in range(4):
        far = lax.rem(micro + ahead, 4)
        for lane in range(2):
            local = 7 + lane
            even_piece = pieces[MOVES.index((ahead, lane)) if ahead else local]
            odd_piece = pieces[MOVES.index((ahead, lane)) if ahead or lane else local]
            z = 2 * far + (half if lane == 0 else 1 - half)
            for j in range(4):
                first = len(even_copies)
                even_copies += block_copies(even_piece.at[j], (4 * lane + j) * 4 + far, first)
                odd_copies += block_copies(odd_piece.at[j], z * 4 + j, first)

    @pl.when(odd == 0)
    def _():
        for copy in even_copies:
            copy.start()

    @pl.when(odd == 1)
    def _():
        for copy in odd_copies:
            copy.start()

    text = text_ref[...].astype(F32)
    mean = jnp.mean(text * text, axis=-1, keepdims=True)
    normed = (text * lax.rsqrt(mean + 1e-06) * gain_ref[...]).astype(BF)
    key_gain = qk_ref[1:2, :]

    @pl.when(odd == 0)
    def _():
        for copy in even_copies:
            copy.wait()

    @pl.when(odd == 1)
    def _():
        for copy in odd_copies:
            copy.wait()

    for b in range(32):
        tail = tails[b].astype(F32)
        stale_key[8 * b : 8 * b + 8, :] = tail[0:8]
        stale_value[8 * b : 8 * b + 8, :] = tail[8:16]
        state[8 * b : 8 * b + 8, :] = tail[16:24]
    sv_ref[...] = stale_value[...].astype(BF)
    state_ref[...] = state[...].astype(BF)
    kv = jnp.dot(normed, w_ref[:, width:], preferred_element_type=F32).astype(BF)
    for h in range(heads):
        cols = slice(h * 128, (h + 1) * 128)
        sk_ref[:, cols] = head_norm(stale_key[:, cols], key_gain).astype(BF)
        tk_ref[:, cols] = head_norm(kv[:, cols].astype(F32), key_gain).astype(BF)
    tv_ref[...] = kv[:, width:]


def layer_kernel(
    heads, flag_ref, patch_ref, text_len_ref, x_ref, w_hbm, gain_ref, qk_ref, tk_ref, tv_ref,
    sk_ref, sv_ref, out_ref, cache_ref, w_ref, sems,
):
    width = heads * 128
    copies = [
        pltpu.make_async_copy(w_hbm.at[:, part], w_ref.at[:, part], sems.at[k])
        for k, part in enumerate((pl.ds(0, width), pl.ds(width, 2 * width)))
    ]
    for copy in copies:
        copy.start()
    section, _, micro, half, side = position()
    stale, limit, text_limit = flag_ref[micro, section] == 1, patch_ref[micro], text_len_ref[0]
    own_ref = x_ref.at[2 * half + side]
    parts = [x_ref[q].astype(F32) for q in range(4)]
    total = sum(jnp.sum(part * part, axis=-1, keepdims=True) for part in parts)
    scale = lax.rsqrt(total / (4 * width) + 1e-06)
    normed = jnp.concatenate(
        [
            (part * scale * gain_ref[:, q * width : (q + 1) * width]).astype(BF)
            for q, part in enumerate(parts)
        ],
        axis=1,
    )
    query_gain, key_gain = qk_ref[0:1, :], qk_ref[1:2, :]
    tokens = out_ref.shape[0]
    own_mask = lax.broadcasted_iota(jnp.int32, (tokens, tokens), 1) < limit
    text_mask = lax.broadcasted_iota(jnp.int32, (tokens, tk_ref.shape[0]), 1) < text_limit
    contract = (((1,), (1,)), ((), ()))
    spans = [slice(h * 128, (h + 1) * 128) for h in range(heads)]
    copies[0].wait()
    projected = jnp.dot(normed, w_ref[:, :width], preferred_element_type=F32)
    queries = [head_norm(projected[:, cols], query_gain).astype(BF) for cols in spans]
    numerators, denominators = [], []
    for h, cols in enumerate(spans):
        text = lax.dot_general(queries[h], tk_ref[:, cols], contract, preferred_element_type=F32)
        text = jnp.where(text_mask, jnp.exp(text * 128 ** (-0.5)), 0.0)
        numerators.append(jnp.dot(text.astype(BF), tv_ref[:, cols], preferred_element_type=F32))
        denominators.append(jnp.sum(text, axis=1, keepdims=True))
    copies[1].wait()
    fresh = jnp.dot(normed, w_ref[:, width:], preferred_element_type=F32).astype(BF)
    cache_ref[0] = fresh[:, :width]
    cache_ref[1] = fresh[:, width:]
    for h, cols in enumerate(spans):
        keys = head_norm(fresh[:, cols].astype(F32), key_gain).astype(BF)
        keys = jnp.where(stale, sk_ref[:, cols], keys)
        values = jnp.where(stale, sv_ref[:, cols], fresh[:, width + h * 128 : width + (h + 1) * 128])
        own = lax.dot_general(queries[h], keys, contract, preferred_element_type=F32)
        own = jnp.where(own_mask, jnp.exp(own * 128 ** (-0.5)), 0.0)
        numerator = numerators[h] + jnp.dot(own.astype(BF), values, preferred_element_type=F32)
        denominator = denominators[h] + jnp.sum(own, axis=1, keepdims=True)
        out_ref[:, cols] = (own_ref[:, cols].astype(F32) + numerator / denominator).astype(BF)


def shards(
    hidden_in, w_qkv, norm_gain, qk_gain, text_states, text_len, patch_len, stale_flags, stale_kv
):
    sections = lax.axis_size("section")
    section = lax.axis_index("section")
    z = lax.axis_index("blk") // 4
    head = lax.axis_index("head")
    odd = section % 2 == 1
    micros, tok, half_width = hidden_in.shape
    width = half_width // 2
    heads = width // 128
    tokens, text_count, depth = 32 * tok, text_states.shape[1], text_states.shape[2]

    w = jnp.moveaxis(w_qkv[0], 1, 0).reshape(3, ROWS, 2, width)
    w = jnp.moveaxis(w, 2, 0).reshape(1, 2, 3 * ROWS, width)
    old = jnp.moveaxis(stale_kv[0].reshape(2, micros, tok, 2, width), (1, 3), (0, 1))
    first = jnp.moveaxis(hidden_in.reshape(micros, tok, 2, width), 2, 1)
    packed = jnp.concatenate(
        [
            jnp.broadcast_to(w, (micros,) + w.shape[1:]),
            old.reshape(micros, 2, 2 * tok, width),
            first,
            jnp.zeros((micros, 2, TAIL - 3 * tok, width), BF),
        ],
        axis=2,
    ).reshape(2 * micros, PIECE, width)
    ring = lax.all_to_all(packed, AX, 0, 0, axis_index_groups=ring_groups(sections), tiled=True)
    by_half = ring.reshape(4, 2, PIECE, width)
    low = z % 2 == 1
    lanes = (
        jnp.where(odd, jnp.where(low, by_half[:, 1], by_half[:, 0]), ring[:4]),
        jnp.where(odd, jnp.where(low, by_half[:, 0], by_half[:, 1]), ring[4:]),
    )
    pieces = [lax.ppermute(lanes[lane], AX, move_pairs(ahead, lane, sections)) for ahead, lane in MOVES]
    pieces = [pltpu.with_memory_space_constraint(piece, pltpu.HBM) for piece in (*pieces, *lanes)]

    qk = qk_gain[0]
    block = jax.ShapeDtypeStruct((tokens, width), BF)
    text_block = jax.ShapeDtypeStruct((text_count, width), BF)
    weights, text_key, text_value, stale_key, stale_value, state = pl.pallas_call(
        functools.partial(prep_kernel, heads),
        out_shape=[jax.ShapeDtypeStruct((depth, 3 * width), BF), text_block, text_block]
        + [block] * 3,
        in_specs=[HBM] * 9 + [VMEM] * 3,
        out_specs=[VMEM] * 6,
        scratch_shapes=[
            pltpu.VMEM((32, TAIL, width), BF),
            pltpu.VMEM((tokens, width), F32),
            pltpu.VMEM((tokens, width), F32),
            pltpu.VMEM((tokens, width), F32),
            pltpu.SemaphoreType.DMA((128,)),
        ],
        compiler_params=pltpu.CompilerParams(vmem_limit_bytes=16 * 2**20),
        name="prepare",
    )(*pieces, text_states[0], norm_gain, qk)

    layer = pl.pallas_call(
        functools.partial(layer_kernel, heads),
        out_shape=[block, jax.ShapeDtypeStruct((2, tokens, width), BF)],
        in_specs=[SMEM] * 3 + [VMEM] + [HBM] + [VMEM] * 6,
        out_specs=[VMEM] * 2,
        scratch_shapes=[pltpu.VMEM((depth, 3 * width), BF), pltpu.SemaphoreType.DMA((2,))],
        compiler_params=pltpu.CompilerParams(vmem_limit_bytes=16 * 2**20),
        name="layer",
    )

    def advance(step, entering):
        whole = lax.all_to_all(
            jnp.broadcast_to(entering[None], (4,) + entering.shape),
            PLANE, 0, 0,
            axis_index_groups=block_groups(step > 0 and step % 2 == 0),
            tiled=True,
        )
        return layer(
            stale_flags, patch_len, text_len, whole, weights, norm_gain, qk, text_key, text_value,
            stale_key, stale_value,
        )

    weights = pltpu.with_memory_space_constraint(weights, pltpu.HBM)
    kept = (state, jnp.zeros((2, tokens, width), BF))
    for step in range(sections):
        entering = lax.ppermute(kept[0], AX, hop_pairs(step - 1)) if step else state
        kept = lax.cond(
            section == step,
            lambda entering, *kept: tuple(advance(step, entering)),
            lambda entering, *kept: tuple(kept),
            entering, *kept,
        )

    result = jnp.concatenate([kept[0][None], kept[1]]).reshape(3, 32, tok, width)
    result = lax.all_to_all(jnp.moveaxis(result, 1, 0), "blk", 0, 0, tiled=True)
    found = [
        jnp.stack([result[(2 * m + j) * 4 + m] for m in range(micros)]) for j in range(2)
    ]
    swap = [
        (at(s, 0, 0) + 2 * b + h, at(s, 0, 0) + 2 * b + 1 - h)
        for s in range(1, sections, 2)
        for b in range(32)
        for h in range(2)
    ]
    other = lax.ppermute(jnp.where(head == 0, found[1], found[0]), AX, swap)
    left = jnp.where(odd & (head == 1), other, found[0])
    right = jnp.where(odd & (head == 0), other, found[1])
    out = jnp.stack([left, right]).transpose(2, 1, 3, 0, 4)
    out = out.reshape(3, micros, tok, half_width)
    return (out[0][None], out[1:][None])


def solution(mesh):
    in_specs = (
        P(None, "blk", "head"),
        P("section", "blk", None, "head"),
        P("section", None),
        P("section", None, None),
        P("section", None, None),
        P(),
        P(),
        P(),
        P("section", None, None, "blk", "head"),
    )
    out_specs = (P("section", None, "blk", "head"), P("section", None, None, "blk", "head"))
    return jax.shard_map(shards, mesh=mesh, in_specs=in_specs, out_specs=out_specs, check_vma=False)
```

```python
import functools
import jax
import jax.numpy as jnp
from jax import lax
from jax.experimental import pallas as pl
from jax.experimental.pallas import tpu as pltpu
from jax.sharding import PartitionSpec as P

AX = ("section", "blk", "head")
PLANE = ("blk", "head")
BF = jnp.bfloat16
F32 = jnp.float32
ROWS = 48
TAIL = 32
PIECE = 3 * ROWS + TAIL
MOVES = [(0, 1), (2, 0), (1, 0), (3, 0), (2, 1), (1, 1), (3, 1)]
HBM = pl.BlockSpec(memory_space=pltpu.HBM)
VMEM = pl.BlockSpec(memory_space=pltpu.VMEM)
SMEM = pl.BlockSpec(memory_space=pltpu.SMEM)


def at(section, z, y):
    return section * 64 + z * 8 + y


def ring_groups(sections):
    groups = []
    for s in range(sections):
        for i in range(8):
            groups.append([at(s, j, i) if s % 2 == 0 else at(s, i, j) for j in range(8)])
    return groups


def move_pairs(ahead, lane, sections):
    even = [
        (at(s, z, (2 * (z // 2 + ahead)) % 8 + half), at(s, z, z // 2 * 2 + half))
        for s in range(0, sections, 2)
        for z in range(8)
        for half in range(2)
    ]
    odd = [
        (at(s, (2 * (y // 2 + ahead)) % 8 + low, y), at(s, y // 2 * 2 + (low ^ lane), y))
        for s in range(1, sections, 2)
        for low in range(2)
        for y in range(8)
    ]
    return odd if ahead == 0 else even + odd


def block_groups(odd):
    order = [(h, q) if odd else (q, h) for h in range(2) for q in range(2)]
    return [[at(0, 2 * i + z, 2 * j + y) for z, y in order] for i in range(4) for j in range(4)]


def hop_pairs(step):
    return [
        (at(step, 2 * m + i, 2 * m + j), at(step + 1, 2 * m + i, 2 * m + j))
        for m in range(4)
        for i in range(2)
        for j in range(2)
    ]


def position():
    section, blk, head = lax.axis_index("section"), lax.axis_index("blk"), lax.axis_index("head")
    z_low = lax.rem(blk // 4, 2)
    odd = lax.rem(section, 2)
    half = jnp.where(odd == 1, z_low, head)
    side = jnp.where(odd == 1, head, z_low)
    return section, odd, blk // 8, half, side


def head_norm(block, gain):
    mean = jnp.mean(block * block, axis=-1, keepdims=True)
    return block * lax.rsqrt(mean + 1e-06) * gain


def pack_kernel(w_ref, stale_ref, hidden_ref, out_ref):
    micros, width = hidden_ref.shape[0], out_ref.shape[2]
    sides = [slice(0, width), slice(width, 2 * width)]
    for m in range(micros):
        states = [hidden_ref[m, :, cols].astype(F32) for cols in sides]
        states = jnp.concatenate(states, axis=0).astype(BF)
        for side, cols in enumerate(sides):
            place = 2 * m + side
            for part in range(3):
                out_ref[place, part * ROWS : (part + 1) * ROWS, :] = w_ref[part, :, cols]
            old = [stale_ref[part, m, :, cols].astype(F32) for part in range(2)]
            old = jnp.concatenate(old, axis=0).astype(BF)
            out_ref[place, 3 * ROWS : 3 * ROWS + 16, :] = old
            out_ref[place, 3 * ROWS + 16 : PIECE, :] = states


def prep_kernel(heads, *refs):
    flag_ref, patch_ref, text_len_ref, text_ref, gain_ref, qk_ref = refs[:6]
    pieces, (w_ref, info_ref), refs = refs[6:15], refs[15:17], refs[17:]
    tk_ref, tv_ref, sk_ref, sv_ref, state_ref = refs[:5]
    tails, held, stale_key, stale_value, state, sems = refs[5:]
    width = heads * 128
    section, odd, micro, half, _ = position()
    line = lax.broadcasted_iota(jnp.int32, info_ref.shape, 0)
    limits = jnp.where(line == 1, patch_ref[micro], text_len_ref[0])
    info_ref[...] = jnp.where(line == 0, flag_ref[micro, section], limits)

    def block_copies(source, block, first):
        row = pl.multiple_of(block * ROWS, 16)
        made = [
            pltpu.make_async_copy(
                source.at[pl.ds(part * ROWS, ROWS), :],
                held.at[pl.ds(row, ROWS), pl.ds(part * width, width)],
                sems.at[first + part],
            )
            for part in range(3)
        ]
        made.append(
            pltpu.make_async_copy(
                source.at[pl.ds(3 * ROWS, TAIL), :], tails.at[block], sems.at[first + 3]
            )
        )
        return made

    even_copies, odd_copies = [], []
    for ahead in range(4):
        far = lax.rem(micro + ahead, 4)
        for lane in range(2):
            local = 7 + lane
            even_piece = pieces[MOVES.index((ahead, lane)) if ahead else local]
            odd_piece = pieces[MOVES.index((ahead, lane)) if ahead or lane else local]
            z = 2 * far + (half if lane == 0 else 1 - half)
            for j in range(4):
                first = len(even_copies)
                even_copies += block_copies(even_piece.at[j], (4 * lane + j) * 4 + far, first)
                odd_copies += block_copies(odd_piece.at[j], z * 4 + j, first)

    @pl.when(odd == 0)
    def _():
        for copy in even_copies:
            copy.start()

    @pl.when(odd == 1)
    def _():
        for copy in odd_copies:
            copy.start()

    text = text_ref[...].astype(F32)
    mean = jnp.mean(text * text, axis=-1, keepdims=True)
    normed = (text * lax.rsqrt(mean + 1e-06) * gain_ref[...]).astype(BF)
    key_gain = qk_ref[1:2, :]

    @pl.when(odd == 0)
    def _():
        for copy in even_copies:
            copy.wait()

    @pl.when(odd == 1)
    def _():
        for copy in odd_copies:
            copy.wait()

    store = pltpu.make_async_copy(held, w_ref, sems.at[128])
    store.start()
    for b in range(32):
        tail = tails[b].astype(F32)
        stale_key[8 * b : 8 * b + 8, :] = tail[0:8]
        stale_value[8 * b : 8 * b + 8, :] = tail[8:16]
        state[0, 8 * b : 8 * b + 8, :] = tail[16:24]
        state[1, 8 * b : 8 * b + 8, :] = tail[24:32]
    sv_ref[...] = stale_value[...].astype(BF)
    state_ref[...] = state[...].astype(BF)
    kv = jnp.dot(normed, held[:, width:], preferred_element_type=F32).astype(BF)
    for h in range(heads):
        cols = slice(h * 128, (h + 1) * 128)
        sk_ref[:, cols] = head_norm(stale_key[:, cols], key_gain).astype(BF)
        tk_ref[:, cols] = head_norm(kv[:, cols].astype(F32), key_gain).astype(BF)
    tv_ref[...] = kv[:, width:]
    store.wait()


def layer_kernel(
    heads, info_ref, x_ref, w_ref, gain_ref, qk_ref, tk_ref, tv_ref,
    sk_ref, sv_ref, out_ref, cache_ref,
):
    width = heads * 128
    _, _, _, half, side = position()
    stale, limit, text_limit = info_ref[0:1, :] == 1, info_ref[1:2, 0:1], info_ref[2:3, 0:1]
    own_ref = x_ref.at[2 * half + side]
    parts = [x_ref[q].astype(F32) for q in range(4)]
    total = sum(jnp.sum(part * part, axis=-1, keepdims=True) for part in parts)
    scale = lax.rsqrt(total / (4 * width) + 1e-06)
    normed = jnp.concatenate(
        [
            (part * scale * gain_ref[:, q * width : (q + 1) * width]).astype(BF)
            for q, part in enumerate(parts)
        ],
        axis=1,
    )
    projected = jnp.dot(normed, w_ref[...], preferred_element_type=F32)
    fresh = projected[:, width:].astype(BF)
    cache_ref[0] = fresh[:, :width]
    cache_ref[1] = fresh[:, width:]
    query_gain, key_gain = qk_ref[0:1, :], qk_ref[1:2, :]
    tokens = out_ref.shape[0]
    own_mask = lax.broadcasted_iota(jnp.int32, (tokens, tokens), 1) < limit
    text_mask = lax.broadcasted_iota(jnp.int32, (tokens, tk_ref.shape[0]), 1) < text_limit
    contract = (((1,), (1,)), ((), ()))
    for h in range(heads):
        cols = slice(h * 128, (h + 1) * 128)
        queries = head_norm(projected[:, cols], query_gain).astype(BF)
        keys = head_norm(fresh[:, cols].astype(F32), key_gain).astype(BF)
        keys = jnp.where(stale, sk_ref[:, cols], keys)
        values = jnp.where(stale, sv_ref[:, cols], fresh[:, width + h * 128 : width + (h + 1) * 128])
        own = lax.dot_general(queries, keys, contract, preferred_element_type=F32)
        own = jnp.where(own_mask, jnp.exp(own * 128 ** (-0.5)), 0.0)
        text = lax.dot_general(queries, tk_ref[:, cols], contract, preferred_element_type=F32)
        text = jnp.where(text_mask, jnp.exp(text * 128 ** (-0.5)), 0.0)
        numerator = jnp.dot(text.astype(BF), tv_ref[:, cols], preferred_element_type=F32)
        numerator += jnp.dot(own.astype(BF), values, preferred_element_type=F32)
        denominator = jnp.sum(own, axis=1, keepdims=True) + jnp.sum(text, axis=1, keepdims=True)
        out_ref[:, cols] = (own_ref[:, cols].astype(F32) + numerator / denominator).astype(BF)


def shards(
    hidden_in, w_qkv, norm_gain, qk_gain, text_states, text_len, patch_len, stale_flags, stale_kv
):
    sections = lax.axis_size("section")
    section = lax.axis_index("section")
    z = lax.axis_index("blk") // 4
    head = lax.axis_index("head")
    odd = section % 2 == 1
    micros, tok, half_width = hidden_in.shape
    width = half_width // 2
    heads = width // 128
    tokens, text_count, depth = 32 * tok, text_states.shape[1], text_states.shape[2]

    sources = [
        pltpu.with_memory_space_constraint(source, pltpu.HBM)
        for source in (jnp.moveaxis(w_qkv[0], 1, 0), stale_kv[0], hidden_in)
    ]
    packed = pl.pallas_call(
        pack_kernel,
        out_shape=jax.ShapeDtypeStruct((2 * micros, PIECE, width), BF),
        in_specs=[VMEM] * 3,
        out_specs=VMEM,
        compiler_params=pltpu.CompilerParams(vmem_limit_bytes=16 * 2**20),
        name="pack",
    )(*sources)
    ring = lax.all_to_all(packed, AX, 0, 0, axis_index_groups=ring_groups(sections), tiled=True)
    by_half = ring.reshape(4, 2, PIECE, width)
    low = z % 2 == 1
    lanes = (
        jnp.where(odd, jnp.where(low, by_half[:, 1], by_half[:, 0]), ring[:4]),
        jnp.where(odd, jnp.where(low, by_half[:, 0], by_half[:, 1]), ring[4:]),
    )
    pieces = [lax.ppermute(lanes[lane], AX, move_pairs(ahead, lane, sections)) for ahead, lane in MOVES]
    pieces = [pltpu.with_memory_space_constraint(piece, pltpu.HBM) for piece in (*pieces, *lanes)]

    qk = qk_gain[0]
    block = jax.ShapeDtypeStruct((tokens, width), BF)
    text_block = jax.ShapeDtypeStruct((text_count, width), BF)
    weights, info, text_key, text_value, stale_key, stale_value, state = pl.pallas_call(
        functools.partial(prep_kernel, heads),
        out_shape=[
            jax.ShapeDtypeStruct((depth, 3 * width), BF),
            jax.ShapeDtypeStruct((8, 128), jnp.int32),
            text_block,
            text_block,
            block,
            block,
            jax.ShapeDtypeStruct((2, tokens, width), BF),
        ],
        in_specs=[SMEM] * 3 + [VMEM] * 3 + [HBM] * 9,
        out_specs=[HBM] + [VMEM] * 6,
        scratch_shapes=[
            pltpu.VMEM((32, TAIL, width), BF),
            pltpu.VMEM((depth, 3 * width), BF),
            pltpu.VMEM((tokens, width), F32),
            pltpu.VMEM((tokens, width), F32),
            pltpu.VMEM((2, tokens, width), F32),
            pltpu.SemaphoreType.DMA((129,)),
        ],
        compiler_params=pltpu.CompilerParams(vmem_limit_bytes=16 * 2**20),
        name="prepare",
    )(stale_flags, patch_len, text_len, text_states[0], norm_gain, qk, *pieces)

    layer = pl.pallas_call(
        functools.partial(layer_kernel, heads),
        out_shape=[block, jax.ShapeDtypeStruct((2, tokens, width), BF)],
        in_specs=[VMEM] * 9,
        out_specs=[VMEM] * 2,
        compiler_params=pltpu.CompilerParams(vmem_limit_bytes=16 * 2**20),
        name="layer",
    )

    weights = pltpu.with_memory_space_constraint(weights, pltpu.HBM)
    rest = (weights, norm_gain, qk, text_key, text_value, stale_key, stale_value)

    def advance(step, entering):
        whole = lax.all_to_all(
            jnp.broadcast_to(entering[None], (4,) + entering.shape),
            PLANE, 0, 0, axis_index_groups=block_groups(step % 2 == 0), tiled=True,
        )
        return tuple(layer(info, whole, *rest))

    whole = lax.all_gather(state, "head", axis=0, tiled=True)
    kept = (jnp.zeros((tokens, width), BF), jnp.zeros((2, tokens, width), BF))
    kept = lax.cond(
        section == 0, lambda whole, *kept: tuple(layer(info, whole, *rest)), lambda whole, *kept: kept,
        whole, *kept,
    )
    for step in range(1, sections):
        entering = lax.ppermute(kept[0], AX, hop_pairs(step - 1))
        kept = lax.cond(
            section == step,
            lambda entering, *kept: advance(step, entering),
            lambda entering, *kept: kept,
            entering, *kept,
        )

    result = jnp.concatenate([kept[0][None], kept[1]]).reshape(3, 32, tok, width)
    result = lax.all_to_all(jnp.moveaxis(result, 1, 0), "blk", 0, 0, tiled=True)
    found = [
        jnp.stack([result[(2 * m + j) * 4 + m] for m in range(micros)]) for j in range(2)
    ]
    swap = [
        (at(s, 0, 0) + 2 * b + h, at(s, 0, 0) + 2 * b + 1 - h)
        for s in range(1, sections, 2)
        for b in range(32)
        for h in range(2)
    ]
    other = lax.ppermute(jnp.where(head == 0, found[1], found[0]), AX, swap)
    left = jnp.where(odd & (head == 1), other, found[0])
    right = jnp.where(odd & (head == 0), other, found[1])
    out = jnp.stack([left, right]).transpose(2, 1, 3, 0, 4)
    out = out.reshape(3, micros, tok, half_width)
    return (out[0][None], out[1:][None])


def solution(mesh):
    in_specs = (
        P(None, "blk", "head"),
        P("section", "blk", None, "head"),
        P("section", None),
        P("section", None, None),
        P("section", None, None),
        P(),
        P(),
        P(),
        P("section", None, None, "blk", "head"),
    )
    out_specs = (P("section", None, "blk", "head"), P("section", None, None, "blk", "head"))
    return jax.shard_map(shards, mesh=mesh, in_specs=in_specs, out_specs=out_specs, check_vma=False)
```

```python
import functools
import jax
import jax.numpy as jnp
from jax import lax
from jax.experimental import pallas as pl
from jax.experimental.pallas import tpu as pltpu
from jax.sharding import PartitionSpec as P

AX = ("section", "blk", "head")
PLANE = ("blk", "head")
BF = jnp.bfloat16
F32 = jnp.float32
ROWS = 48
TAIL = 32
PIECE = 3 * ROWS + TAIL
MOVES = [(0, 1), (2, 0), (1, 0), (3, 0), (2, 1), (1, 1), (3, 1)]
HBM = pl.BlockSpec(memory_space=pltpu.HBM)
VMEM = pl.BlockSpec(memory_space=pltpu.VMEM)
SMEM = pl.BlockSpec(memory_space=pltpu.SMEM)


def at(section, z, y):
    return section * 64 + z * 8 + y


def ring_groups(sections):
    groups = []
    for s in range(sections):
        for i in range(8):
            groups.append([at(s, j, i) if s % 2 == 0 else at(s, i, j) for j in range(7, -1, -1)])
    return groups


def move_pairs(ahead, lane, sections):
    even = [
        (at(s, z, (2 * (z // 2 + ahead)) % 8 + half), at(s, z, z // 2 * 2 + half))
        for s in range(0, sections, 2)
        for z in range(8)
        for half in range(2)
    ]
    odd = [
        (at(s, (2 * (y // 2 + ahead)) % 8 + low, y), at(s, y // 2 * 2 + (low ^ lane), y))
        for s in range(1, sections, 2)
        for low in range(2)
        for y in range(8)
    ]
    return odd if ahead == 0 else even + odd


def block_groups(odd):
    order = [(h, q) if odd else (q, h) for h in range(2) for q in range(2)]
    return [[at(0, 2 * i + z, 2 * j + y) for z, y in order] for i in range(4) for j in range(4)]


def pair_pairs():
    return [
        (at(0, 2 * m + i, 2 * m + j), at(0, 2 * m + i, 2 * m + 1 - j))
        for m in range(4)
        for i in range(2)
        for j in range(2)
    ]


def hop_pairs(step):
    return [
        (at(step, 2 * m + i, 2 * m + j), at(step + 1, 2 * m + i, 2 * m + j))
        for m in range(4)
        for i in range(2)
        for j in range(2)
    ]


def position():
    section, blk, head = lax.axis_index("section"), lax.axis_index("blk"), lax.axis_index("head")
    z_low = lax.rem(blk // 4, 2)
    odd = lax.rem(section, 2)
    half = jnp.where(odd == 1, z_low, head)
    side = jnp.where(odd == 1, head, z_low)
    return section, odd, blk // 8, half, side


def head_norm(block, gain):
    mean = jnp.mean(block * block, axis=-1, keepdims=True)
    return block * lax.rsqrt(mean + 1e-06) * gain


def pack_kernel(w_ref, stale_ref, hidden_ref, out_ref):
    micros, width = hidden_ref.shape[0], out_ref.shape[2]
    sides = [slice(0, width), slice(width, 2 * width)]
    for m in range(micros):
        states = [hidden_ref[m, :, cols].astype(F32) for cols in sides]
        states = jnp.concatenate(states, axis=0).astype(BF)
        for side, cols in enumerate(sides):
            place = 2 * micros - 1 - (2 * m + side)
            for part in range(3):
                out_ref[place, part * ROWS : (part + 1) * ROWS, :] = w_ref[part, :, cols]
            old = [stale_ref[part, m, :, cols].astype(F32) for part in range(2)]
            old = jnp.concatenate(old, axis=0).astype(BF)
            out_ref[place, 3 * ROWS : 3 * ROWS + 16, :] = old
            out_ref[place, 3 * ROWS + 16 : PIECE, :] = states


def with_blocks(pieces, act):
    _, odd, micro, half, _ = position()
    evens, odds = [], []
    for ahead in range(4):
        far = lax.rem(micro + ahead, 4)
        for lane in range(2):
            local = 7 + lane
            even_piece = pieces[MOVES.index((ahead, lane)) if ahead else local]
            odd_piece = pieces[MOVES.index((ahead, lane)) if ahead or lane else local]
            z = 2 * far + (half if lane == 0 else 1 - half)
            for j in range(4):
                evens.append((even_piece.at[j], (7 - 4 * lane - j) * 4 + far))
                odds.append((odd_piece.at[j], z * 4 + 3 - j))
    for parity, blocks in enumerate((evens, odds)):

        @pl.when(odd == parity)
        def _(blocks=blocks):
            for i, (source, block) in enumerate(blocks):
                act(i, source, block)


def tail_kernel(heads, *refs):
    flag_ref, patch_ref, text_len_ref, qk_ref = refs[:4]
    pieces, (info_ref, sk_ref, sv_ref, state_ref) = refs[4:13], refs[13:17]
    tails, stale_key, stale_value, state, sems = refs[17:]
    section, _, micro, _, _ = position()

    def tail_copy(i, source, block):
        return pltpu.make_async_copy(
            source.at[pl.ds(3 * ROWS, TAIL), :], tails.at[block], sems.at[i]
        )

    with_blocks(pieces, lambda *block: tail_copy(*block).start())
    line = lax.broadcasted_iota(jnp.int32, info_ref.shape, 0)
    limits = jnp.where(line == 1, patch_ref[micro], text_len_ref[0])
    info_ref[...] = jnp.where(line == 0, flag_ref[micro, section], limits)
    with_blocks(pieces, lambda *block: tail_copy(*block).wait())
    for b in range(32):
        tail = tails[b].astype(F32)
        stale_key[8 * b : 8 * b + 8, :] = tail[0:8]
        stale_value[8 * b : 8 * b + 8, :] = tail[8:16]
        state[0, 8 * b : 8 * b + 8, :] = tail[16:24]
        state[1, 8 * b : 8 * b + 8, :] = tail[24:32]
    sv_ref[...] = stale_value[...].astype(BF)
    state_ref[...] = state[...].astype(BF)
    for h in range(heads):
        cols = slice(h * 128, (h + 1) * 128)
        sk_ref[:, cols] = head_norm(stale_key[:, cols], qk_ref[1:2, :]).astype(BF)


def prep_kernel(heads, *refs):
    text_ref, gain_ref, qk_ref = refs[:3]
    pieces, (w_ref, tk_ref, tv_ref), (held, sems) = refs[3:12], refs[12:15], refs[15:]
    width = heads * 128

    def weight_copies(i, source, block):
        row = pl.multiple_of(block * ROWS, 16)
        return [
            pltpu.make_async_copy(
                source.at[pl.ds(part * ROWS, ROWS), :],
                held.at[pl.ds(row, ROWS), pl.ds(part * width, width)],
                sems.at[3 * i + part],
            )
            for part in range(3)
        ]

    with_blocks(pieces, lambda *block: [copy.start() for copy in weight_copies(*block)])
    text = text_ref[...].astype(F32)
    mean = jnp.mean(text * text, axis=-1, keepdims=True)
    normed = (text * lax.rsqrt(mean + 1e-06) * gain_ref[...]).astype(BF)
    with_blocks(pieces, lambda *block: [copy.wait() for copy in weight_copies(*block)])
    store = pltpu.make_async_copy(held, w_ref, sems.at[96])
    store.start()
    kv = jnp.dot(normed, held[:, width:], preferred_element_type=F32).astype(BF)
    for h in range(heads):
        cols = slice(h * 128, (h + 1) * 128)
        tk_ref[:, cols] = head_norm(kv[:, cols].astype(F32), qk_ref[1:2, :]).astype(BF)
    tv_ref[...] = kv[:, width:]
    store.wait()


def layer_kernel(
    heads, info_ref, x_ref, w_ref, gain_ref, qk_ref, tk_ref, tv_ref,
    sk_ref, sv_ref, out_ref, cache_ref,
):
    width = heads * 128
    _, _, _, half, side = position()
    stale, limit, text_limit = info_ref[0:1, :] == 1, info_ref[1:2, 0:1], info_ref[2:3, 0:1]
    own_ref = x_ref.at[2 * half + side]
    parts = [x_ref[q].astype(F32) for q in range(4)]
    total = sum(jnp.sum(part * part, axis=-1, keepdims=True) for part in parts)
    scale = lax.rsqrt(total / (4 * width) + 1e-06)
    normed = jnp.concatenate(
        [
            (part * scale * gain_ref[:, q * width : (q + 1) * width]).astype(BF)
            for q, part in enumerate(parts)
        ],
        axis=1,
    )
    projected = jnp.dot(normed, w_ref[...], preferred_element_type=F32)
    fresh = projected[:, width:].astype(BF)
    cache_ref[0] = fresh[:, :width]
    cache_ref[1] = fresh[:, width:]
    query_gain, key_gain = qk_ref[0:1, :], qk_ref[1:2, :]
    tokens = out_ref.shape[0]
    own_mask = lax.broadcasted_iota(jnp.int32, (tokens, tokens), 1) < limit
    text_mask = lax.broadcasted_iota(jnp.int32, (tokens, tk_ref.shape[0]), 1) < text_limit
    contract = (((1,), (1,)), ((), ()))
    for h in range(heads):
        cols = slice(h * 128, (h + 1) * 128)
        queries = head_norm(projected[:, cols], query_gain).astype(BF)
        keys = head_norm(fresh[:, cols].astype(F32), key_gain).astype(BF)
        keys = jnp.where(stale, sk_ref[:, cols], keys)
        values = jnp.where(stale, sv_ref[:, cols], fresh[:, width + h * 128 : width + (h + 1) * 128])
        own = lax.dot_general(queries, keys, contract, preferred_element_type=F32)
        own = jnp.where(own_mask, jnp.exp(own * 128 ** (-0.5)), 0.0)
        text = lax.dot_general(queries, tk_ref[:, cols], contract, preferred_element_type=F32)
        text = jnp.where(text_mask, jnp.exp(text * 128 ** (-0.5)), 0.0)
        numerator = jnp.dot(text.astype(BF), tv_ref[:, cols], preferred_element_type=F32)
        numerator += jnp.dot(own.astype(BF), values, preferred_element_type=F32)
        denominator = jnp.sum(own, axis=1, keepdims=True) + jnp.sum(text, axis=1, keepdims=True)
        out_ref[:, cols] = (own_ref[:, cols].astype(F32) + numerator / denominator).astype(BF)


def shards(
    hidden_in, w_qkv, norm_gain, qk_gain, text_states, text_len, patch_len, stale_flags, stale_kv
):
    sections = lax.axis_size("section")
    section = lax.axis_index("section")
    z = lax.axis_index("blk") // 4
    head = lax.axis_index("head")
    odd = section % 2 == 1
    micros, tok, half_width = hidden_in.shape
    width = half_width // 2
    heads = width // 128
    tokens, text_count, depth = 32 * tok, text_states.shape[1], text_states.shape[2]

    sources = [
        pltpu.with_memory_space_constraint(source, pltpu.HBM)
        for source in (jnp.moveaxis(w_qkv[0], 1, 0), stale_kv[0], hidden_in)
    ]
    packed = pl.pallas_call(
        pack_kernel,
        out_shape=jax.ShapeDtypeStruct((2 * micros, PIECE, width), BF),
        in_specs=[VMEM] * 3,
        out_specs=VMEM,
        compiler_params=pltpu.CompilerParams(vmem_limit_bytes=16 * 2**20),
        name="pack",
    )(*sources)
    ring = lax.all_to_all(packed, AX, 0, 0, axis_index_groups=ring_groups(sections), tiled=True)
    by_half = ring.reshape(4, 2, PIECE, width)
    low = z % 2 == 1
    lanes = (
        jnp.where(odd, jnp.where(low, by_half[:, 0], by_half[:, 1]), ring[:4]),
        jnp.where(odd, jnp.where(low, by_half[:, 1], by_half[:, 0]), ring[4:]),
    )
    pieces = [lax.ppermute(lanes[lane], AX, move_pairs(ahead, lane, sections)) for ahead, lane in MOVES]
    pieces = [pltpu.with_memory_space_constraint(piece, pltpu.HBM) for piece in (*pieces, *lanes)]

    qk = qk_gain[0]
    block = jax.ShapeDtypeStruct((tokens, width), BF)
    text_block = jax.ShapeDtypeStruct((text_count, width), BF)
    info, stale_key, stale_value, state = pl.pallas_call(
        functools.partial(tail_kernel, heads),
        out_shape=[
            jax.ShapeDtypeStruct((8, 128), jnp.int32),
            block,
            block,
            jax.ShapeDtypeStruct((2, tokens, width), BF),
        ],
        in_specs=[SMEM] * 3 + [VMEM] + [HBM] * 9,
        out_specs=[VMEM] * 4,
        scratch_shapes=[
            pltpu.VMEM((32, TAIL, width), BF),
            pltpu.VMEM((tokens, width), F32),
            pltpu.VMEM((tokens, width), F32),
            pltpu.VMEM((2, tokens, width), F32),
            pltpu.SemaphoreType.DMA((32,)),
        ],
        compiler_params=pltpu.CompilerParams(vmem_limit_bytes=16 * 2**20),
        name="tails",
    )(stale_flags, patch_len, text_len, qk, *pieces)
    other = lax.ppermute(state, AX, pair_pairs())
    weights, text_key, text_value = pl.pallas_call(
        functools.partial(prep_kernel, heads),
        out_shape=[jax.ShapeDtypeStruct((depth, 3 * width), BF), text_block, text_block],
        in_specs=[VMEM] * 3 + [HBM] * 9,
        out_specs=[HBM] + [VMEM] * 2,
        scratch_shapes=[pltpu.VMEM((depth, 3 * width), BF), pltpu.SemaphoreType.DMA((97,))],
        compiler_params=pltpu.CompilerParams(vmem_limit_bytes=16 * 2**20),
        cost_estimate=pl.CostEstimate(
            flops=4 * text_count * depth * width,
            bytes_accessed=12 * depth * width,
            transcendentals=0,
        ),
        name="prepare",
    )(text_states[0], norm_gain, qk, *pieces)
    whole = jnp.where(
        head == 0, jnp.concatenate([state, other]), jnp.concatenate([other, state])
    )

    layer = pl.pallas_call(
        functools.partial(layer_kernel, heads),
        out_shape=[block, jax.ShapeDtypeStruct((2, tokens, width), BF)],
        in_specs=[VMEM] * 9,
        out_specs=[VMEM] * 2,
        compiler_params=pltpu.CompilerParams(vmem_limit_bytes=16 * 2**20),
        name="layer",
    )

    weights = pltpu.with_memory_space_constraint(weights, pltpu.HBM)
    rest = (weights, norm_gain, qk, text_key, text_value, stale_key, stale_value)

    def advance(step, entering):
        whole = lax.all_to_all(
            jnp.broadcast_to(entering[None], (4,) + entering.shape),
            PLANE, 0, 0, axis_index_groups=block_groups(step % 2 == 0), tiled=True,
        )
        return tuple(layer(info, whole, *rest))

    kept = (jnp.zeros((tokens, width), BF), jnp.zeros((2, tokens, width), BF))
    kept = lax.cond(
        section == 0, lambda whole, *kept: tuple(layer(info, whole, *rest)), lambda whole, *kept: kept,
        whole, *kept,
    )
    for step in range(1, sections):
        entering = lax.ppermute(kept[0], AX, hop_pairs(step - 1))
        kept = lax.cond(
            section == step,
            lambda entering, *kept: advance(step, entering),
            lambda entering, *kept: kept,
            entering, *kept,
        )

    result = jnp.concatenate([kept[0][None], kept[1]]).reshape(3, 32, tok, width)
    result = lax.all_to_all(jnp.moveaxis(result, 1, 0), "blk", 0, 0, tiled=True)
    found = [
        jnp.stack([result[(2 * m + j) * 4 + m] for m in range(micros)]) for j in range(2)
    ]
    swap = [
        (at(s, 0, 0) + 2 * b + h, at(s, 0, 0) + 2 * b + 1 - h)
        for s in range(1, sections, 2)
        for b in range(32)
        for h in range(2)
    ]
    other = lax.ppermute(jnp.where(head == 0, found[1], found[0]), AX, swap)
    left = jnp.where(odd & (head == 1), other, found[0])
    right = jnp.where(odd & (head == 0), other, found[1])
    out = jnp.stack([left, right]).transpose(2, 1, 3, 0, 4)
    out = out.reshape(3, micros, tok, half_width)
    return (out[0][None], out[1:][None])


def solution(mesh):
    in_specs = (
        P(None, "blk", "head"),
        P("section", "blk", None, "head"),
        P("section", None),
        P("section", None, None),
        P("section", None, None),
        P(),
        P(),
        P(),
        P("section", None, None, "blk", "head"),
    )
    out_specs = (P("section", None, "blk", "head"), P("section", None, None, "blk", "head"))
    return jax.shard_map(shards, mesh=mesh, in_specs=in_specs, out_specs=out_specs, check_vma=False)
```

```python
import functools
import jax
import jax.numpy as jnp
from jax import lax
from jax.experimental import pallas as pl
from jax.experimental.pallas import tpu as pltpu
from jax.sharding import PartitionSpec as P

AX = ("section", "blk", "head")
PLANE = ("blk", "head")
BF = jnp.bfloat16
F32 = jnp.float32
ROWS = 48
TAIL = 32
PIECE = 3 * ROWS + TAIL
MOVES = [(0, 1), (2, 0), (1, 0), (3, 0), (2, 1), (1, 1), (3, 1)]
HBM = pl.BlockSpec(memory_space=pltpu.HBM)
VMEM = pl.BlockSpec(memory_space=pltpu.VMEM)
SMEM = pl.BlockSpec(memory_space=pltpu.SMEM)


def at(section, z, y):
    return section * 64 + z * 8 + y


def ring_groups(sections):
    groups = []
    for s in range(sections):
        for i in range(8):
            groups.append([at(s, j, i) if s % 2 == 0 else at(s, i, j) for j in range(7, -1, -1)])
    return groups


def move_pairs(ahead, lane, sections):
    even = [
        (at(s, z, (2 * (z // 2 + ahead)) % 8 + half), at(s, z, z // 2 * 2 + half))
        for s in range(0, sections, 2)
        for z in range(8)
        for half in range(2)
    ]
    odd = [
        (at(s, (2 * (y // 2 + ahead)) % 8 + low, y), at(s, y // 2 * 2 + (low ^ lane), y))
        for s in range(1, sections, 2)
        for low in range(2)
        for y in range(8)
    ]
    return odd if ahead == 0 else even + odd


def block_groups(odd):
    order = [(h, q) if odd else (q, h) for h in range(2) for q in range(2)]
    return [[at(0, 2 * i + z, 2 * j + y) for z, y in order] for i in range(4) for j in range(4)]


def pair_pairs():
    return [
        (at(0, 2 * m + i, 2 * m + j), at(0, 2 * m + i, 2 * m + 1 - j))
        for m in range(4)
        for i in range(2)
        for j in range(2)
    ]


def hop_pairs(step):
    return [
        (at(step, 2 * m + i, 2 * m + j), at(step + 1, 2 * m + i, 2 * m + j))
        for m in range(4)
        for i in range(2)
        for j in range(2)
    ]


def position():
    section, blk, head = lax.axis_index("section"), lax.axis_index("blk"), lax.axis_index("head")
    z_low = lax.rem(blk // 4, 2)
    odd = lax.rem(section, 2)
    half = jnp.where(odd == 1, z_low, head)
    side = jnp.where(odd == 1, head, z_low)
    return section, odd, blk // 8, half, side


def head_norm(block, gain):
    mean = jnp.mean(block * block, axis=-1, keepdims=True)
    return block * lax.rsqrt(mean + 1e-06) * gain


def pack_kernel(w_ref, stale_ref, hidden_ref, out_ref):
    micros, width = hidden_ref.shape[0], out_ref.shape[2]
    sides = [slice(0, width), slice(width, 2 * width)]
    for m in range(micros):
        states = [hidden_ref[m, :, cols].astype(F32) for cols in sides]
        states = jnp.concatenate(states, axis=0).astype(BF)
        for side, cols in enumerate(sides):
            place = 2 * micros - 1 - (2 * m + side)
            for part in range(3):
                out_ref[place, part * ROWS : (part + 1) * ROWS, :] = w_ref[part, :, cols]
            old = [stale_ref[part, m, :, cols].astype(F32) for part in range(2)]
            old = jnp.concatenate(old, axis=0).astype(BF)
            out_ref[place, 3 * ROWS : 3 * ROWS + 16, :] = old
            out_ref[place, 3 * ROWS + 16 : PIECE, :] = states


def with_blocks(pieces, act):
    _, odd, micro, half, _ = position()
    evens, odds = [], []
    for ahead in range(4):
        far = lax.rem(micro + ahead, 4)
        for lane in range(2):
            local = 7 + lane
            even_piece = pieces[MOVES.index((ahead, lane)) if ahead else local]
            odd_piece = pieces[MOVES.index((ahead, lane)) if ahead or lane else local]
            z = 2 * far + (half if lane == 0 else 1 - half)
            for j in range(4):
                evens.append((even_piece.at[j], (7 - 4 * lane - j) * 4 + far))
                odds.append((odd_piece.at[j], z * 4 + 3 - j))
    for parity, blocks in enumerate((evens, odds)):

        @pl.when(odd == parity)
        def _(blocks=blocks):
            for i, (source, block) in enumerate(blocks):
                act(i, source, block)


def tail_kernel(heads, *refs):
    flag_ref, patch_ref, text_len_ref, qk_ref = refs[:4]
    pieces, (info_ref, sk_ref, sv_ref, state_ref) = refs[4:13], refs[13:17]
    tails, stale_key, stale_value, state, sems = refs[17:]
    section, _, micro, _, _ = position()

    def tail_copy(i, source, block):
        return pltpu.make_async_copy(
            source.at[pl.ds(3 * ROWS, TAIL), :], tails.at[block], sems.at[i]
        )

    with_blocks(pieces, lambda *block: tail_copy(*block).start())
    line = lax.broadcasted_iota(jnp.int32, info_ref.shape, 0)
    limits = jnp.where(line == 1, patch_ref[micro], text_len_ref[0])
    info_ref[...] = jnp.where(line == 0, flag_ref[micro, section], limits)
    with_blocks(pieces, lambda *block: tail_copy(*block).wait())
    for b in range(32):
        tail = tails[b].astype(F32)
        stale_key[8 * b : 8 * b + 8, :] = tail[0:8]
        stale_value[8 * b : 8 * b + 8, :] = tail[8:16]
        state[0, 8 * b : 8 * b + 8, :] = tail[16:24]
        state[1, 8 * b : 8 * b + 8, :] = tail[24:32]
    sv_ref[...] = stale_value[...].astype(BF)
    state_ref[...] = state[...].astype(BF)
    for h in range(heads):
        cols = slice(h * 128, (h + 1) * 128)
        sk_ref[:, cols] = head_norm(stale_key[:, cols], qk_ref[1:2, :]).astype(BF)


def prep_kernel(heads, *refs):
    text_ref, gain_ref, qk_ref = refs[:3]
    pieces, (w_ref, tk_ref, tv_ref), (held, sems) = refs[3:12], refs[12:15], refs[15:]
    width = heads * 128

    def weight_copies(i, source, block):
        row = pl.multiple_of(block * ROWS, 16)
        return [
            pltpu.make_async_copy(
                source.at[pl.ds(part * ROWS, ROWS), :],
                held.at[pl.ds(row, ROWS), pl.ds(part * width, width)],
                sems.at[3 * i + part],
            )
            for part in range(3)
        ]

    with_blocks(pieces, lambda *block: [copy.start() for copy in weight_copies(*block)])
    text = text_ref[...].astype(F32)
    mean = jnp.mean(text * text, axis=-1, keepdims=True)
    normed = (text * lax.rsqrt(mean + 1e-06) * gain_ref[...]).astype(BF)
    with_blocks(pieces, lambda *block: [copy.wait() for copy in weight_copies(*block)])
    store = pltpu.make_async_copy(held, w_ref, sems.at[96])
    store.start()
    kv = jnp.dot(normed, held[:, width:], preferred_element_type=F32).astype(BF)
    for h in range(heads):
        cols = slice(h * 128, (h + 1) * 128)
        tk_ref[:, cols] = head_norm(kv[:, cols].astype(F32), qk_ref[1:2, :]).astype(BF)
    tv_ref[...] = kv[:, width:]
    store.wait()


def layer_kernel(
    heads, info_ref, x_ref, w_ref, gain_ref, qk_ref, tk_ref, tv_ref,
    sk_ref, sv_ref, out_ref, cache_ref,
):
    width = heads * 128
    _, _, _, half, side = position()
    stale, limit, text_limit = info_ref[0:1, :] == 1, info_ref[1:2, 0:1], info_ref[2:3, 0:1]
    own_ref = x_ref.at[2 * half + side]
    parts = [x_ref[q].astype(F32) for q in range(4)]
    total = sum(jnp.sum(part * part, axis=-1, keepdims=True) for part in parts)
    scale = lax.rsqrt(total / (4 * width) + 1e-06)
    normed = jnp.concatenate(
        [
            (part * scale * gain_ref[:, q * width : (q + 1) * width]).astype(BF)
            for q, part in enumerate(parts)
        ],
        axis=1,
    )
    projected = jnp.dot(normed, w_ref[...], preferred_element_type=F32)
    fresh = projected[:, width:].astype(BF)
    cache_ref[0] = fresh[:, :width]
    cache_ref[1] = fresh[:, width:]
    query_gain, key_gain = qk_ref[0:1, :], qk_ref[1:2, :]
    tokens = out_ref.shape[0]
    own_mask = lax.broadcasted_iota(jnp.int32, (tokens, tokens), 1) < limit
    text_mask = lax.broadcasted_iota(jnp.int32, (tokens, tk_ref.shape[0]), 1) < text_limit
    contract = (((1,), (1,)), ((), ()))
    for h in range(heads):
        cols = slice(h * 128, (h + 1) * 128)
        queries = head_norm(projected[:, cols], query_gain).astype(BF)
        keys = head_norm(fresh[:, cols].astype(F32), key_gain).astype(BF)
        keys = jnp.where(stale, sk_ref[:, cols], keys)
        values = jnp.where(stale, sv_ref[:, cols], fresh[:, width + h * 128 : width + (h + 1) * 128])
        own = lax.dot_general(queries, keys, contract, preferred_element_type=F32)
        own = jnp.where(own_mask, jnp.exp(own * 128 ** (-0.5)), 0.0)
        text = lax.dot_general(queries, tk_ref[:, cols], contract, preferred_element_type=F32)
        text = jnp.where(text_mask, jnp.exp(text * 128 ** (-0.5)), 0.0)
        numerator = jnp.dot(text.astype(BF), tv_ref[:, cols], preferred_element_type=F32)
        numerator += jnp.dot(own.astype(BF), values, preferred_element_type=F32)
        denominator = jnp.sum(own, axis=1, keepdims=True) + jnp.sum(text, axis=1, keepdims=True)
        out_ref[:, cols] = (own_ref[:, cols].astype(F32) + numerator / denominator).astype(BF)


def shards(
    hidden_in, w_qkv, norm_gain, qk_gain, text_states, text_len, patch_len, stale_flags, stale_kv
):
    sections = lax.axis_size("section")
    section = lax.axis_index("section")
    z = lax.axis_index("blk") // 4
    head = lax.axis_index("head")
    odd = section % 2 == 1
    micros, tok, half_width = hidden_in.shape
    width = half_width // 2
    heads = width // 128
    tokens, text_count, depth = 32 * tok, text_states.shape[1], text_states.shape[2]

    sources = [
        pltpu.with_memory_space_constraint(source, pltpu.HBM)
        for source in (jnp.moveaxis(w_qkv[0], 1, 0), stale_kv[0], hidden_in)
    ]
    packed = pl.pallas_call(
        pack_kernel,
        out_shape=jax.ShapeDtypeStruct((2 * micros, PIECE, width), BF),
        in_specs=[VMEM] * 3,
        out_specs=VMEM,
        compiler_params=pltpu.CompilerParams(vmem_limit_bytes=16 * 2**20),
        name="pack",
    )(*sources)
    ring = lax.all_to_all(packed, AX, 0, 0, axis_index_groups=ring_groups(sections), tiled=True)
    by_half = ring.reshape(4, 2, PIECE, width)
    low = z % 2 == 1
    lanes = (
        jnp.where(odd, jnp.where(low, by_half[:, 0], by_half[:, 1]), ring[:4]),
        jnp.where(odd, jnp.where(low, by_half[:, 1], by_half[:, 0]), ring[4:]),
    )
    pieces = [lax.ppermute(lanes[lane], AX, move_pairs(ahead, lane, sections)) for ahead, lane in MOVES]
    pieces = [
        *[pltpu.with_memory_space_constraint(piece, pltpu.HBM) for piece in pieces[:-2]],
        *pieces[-2:],
        *[pltpu.with_memory_space_constraint(lane, pltpu.HBM) for lane in lanes],
    ]

    qk = qk_gain[0]
    block = jax.ShapeDtypeStruct((tokens, width), BF)
    text_block = jax.ShapeDtypeStruct((text_count, width), BF)
    info, stale_key, stale_value, state = pl.pallas_call(
        functools.partial(tail_kernel, heads),
        out_shape=[
            jax.ShapeDtypeStruct((8, 128), jnp.int32),
            block,
            block,
            jax.ShapeDtypeStruct((2, tokens, width), BF),
        ],
        in_specs=[SMEM] * 3 + [VMEM] + [HBM] * 9,
        out_specs=[VMEM] * 4,
        scratch_shapes=[
            pltpu.VMEM((32, TAIL, width), BF),
            pltpu.VMEM((tokens, width), F32),
            pltpu.VMEM((tokens, width), F32),
            pltpu.VMEM((2, tokens, width), F32),
            pltpu.SemaphoreType.DMA((32,)),
        ],
        compiler_params=pltpu.CompilerParams(vmem_limit_bytes=16 * 2**20),
        name="tails",
    )(stale_flags, patch_len, text_len, qk, *pieces)
    other = lax.ppermute(state, AX, pair_pairs())
    weights, text_key, text_value = pl.pallas_call(
        functools.partial(prep_kernel, heads),
        out_shape=[jax.ShapeDtypeStruct((depth, 3 * width), BF), text_block, text_block],
        in_specs=[VMEM] * 3 + [HBM] * 9,
        out_specs=[HBM] + [VMEM] * 2,
        scratch_shapes=[pltpu.VMEM((depth, 3 * width), BF), pltpu.SemaphoreType.DMA((97,))],
        compiler_params=pltpu.CompilerParams(vmem_limit_bytes=16 * 2**20),
        cost_estimate=pl.CostEstimate(
            flops=4 * text_count * depth * width,
            bytes_accessed=12 * depth * width,
            transcendentals=0,
        ),
        name="prepare",
    )(text_states[0], norm_gain, qk, *pieces)
    whole = jnp.where(
        head == 0, jnp.concatenate([state, other]), jnp.concatenate([other, state])
    )

    layer = pl.pallas_call(
        functools.partial(layer_kernel, heads),
        out_shape=[block, jax.ShapeDtypeStruct((2, tokens, width), BF)],
        in_specs=[VMEM] * 9,
        out_specs=[VMEM] * 2,
        compiler_params=pltpu.CompilerParams(vmem_limit_bytes=16 * 2**20),
        name="layer",
    )

    weights = pltpu.with_memory_space_constraint(weights, pltpu.HBM)
    rest = (weights, norm_gain, qk, text_key, text_value, stale_key, stale_value)

    def advance(step, entering):
        whole = lax.all_to_all(
            jnp.broadcast_to(entering[None], (4,) + entering.shape),
            PLANE, 0, 0, axis_index_groups=block_groups(step % 2 == 0), tiled=True,
        )
        return tuple(layer(info, whole, *rest))

    kept = (jnp.zeros((tokens, width), BF), jnp.zeros((2, tokens, width), BF))
    kept = lax.cond(
        section == 0, lambda whole, *kept: tuple(layer(info, whole, *rest)), lambda whole, *kept: kept,
        whole, *kept,
    )
    for step in range(1, sections):
        entering = lax.ppermute(kept[0], AX, hop_pairs(step - 1))
        kept = lax.cond(
            section == step,
            lambda entering, *kept: advance(step, entering),
            lambda entering, *kept: kept,
            entering, *kept,
        )

    result = jnp.concatenate([kept[0][None], kept[1]]).reshape(3, 32, tok, width)
    result = lax.all_to_all(jnp.moveaxis(result, 1, 0), "blk", 0, 0, tiled=True)
    found = [
        jnp.stack([result[(2 * m + j) * 4 + m] for m in range(micros)]) for j in range(2)
    ]
    swap = [
        (at(s, 0, 0) + 2 * b + h, at(s, 0, 0) + 2 * b + 1 - h)
        for s in range(1, sections, 2)
        for b in range(32)
        for h in range(2)
    ]
    other = lax.ppermute(jnp.where(head == 0, found[1], found[0]), AX, swap)
    left = jnp.where(odd & (head == 1), other, found[0])
    right = jnp.where(odd & (head == 0), other, found[1])
    sides = jnp.stack([left, right])
    hidden = sides[:, :, 0].transpose(1, 2, 0, 3).reshape(1, micros, tok, half_width)
    cache = sides[:, :, 1:].transpose(2, 1, 3, 0, 4).reshape(1, 2, micros, tok, half_width)
    return (hidden, cache)


def solution(mesh):
    in_specs = (
        P(None, "blk", "head"),
        P("section", "blk", None, "head"),
        P("section", None),
        P("section", None, None),
        P("section", None, None),
        P(),
        P(),
        P(),
        P("section", None, None, "blk", "head"),
    )
    out_specs = (P("section", None, "blk", "head"), P("section", None, None, "blk", "head"))
    return jax.shard_map(shards, mesh=mesh, in_specs=in_specs, out_specs=out_specs, check_vma=False)
```

```python
import functools
import jax
import jax.numpy as jnp
from jax import lax
from jax.experimental import pallas as pl
from jax.experimental.pallas import tpu as pltpu
from jax.sharding import PartitionSpec as P

AX = ("section", "blk", "head")
PLANE = ("blk", "head")
BF = jnp.bfloat16
F32 = jnp.float32
ROWS = 48
TAIL = 32
PIECE = 3 * ROWS + TAIL
MOVES = [(2, 0), (2, 1), (0, 1), (1, 0), (1, 1), (3, 0), (3, 1)]
HBM = pl.BlockSpec(memory_space=pltpu.HBM)
VMEM = pl.BlockSpec(memory_space=pltpu.VMEM)
SMEM = pl.BlockSpec(memory_space=pltpu.SMEM)


def at(section, z, y):
    return section * 64 + z * 8 + y


def ring_groups(sections):
    groups = []
    for s in range(sections):
        for i in range(8):
            groups.append([at(s, j, i) if s % 2 == 0 else at(s, i, j) for j in range(7, -1, -1)])
    return groups


def move_pairs(ahead, lane, sections):
    even = [
        (at(s, z, (2 * (z // 2 + ahead)) % 8 + half), at(s, z, z // 2 * 2 + half))
        for s in range(0, sections, 2)
        for z in range(8)
        for half in range(2)
    ]
    odd = [
        (at(s, (2 * (y // 2 + ahead)) % 8 + low, y), at(s, y // 2 * 2 + (low ^ lane), y))
        for s in range(1, sections, 2)
        for low in range(2)
        for y in range(8)
    ]
    return odd if ahead == 0 else even + odd


def block_groups(odd):
    order = [(h, q) if odd else (q, h) for h in range(2) for q in range(2)]
    return [[at(0, 2 * i + z, 2 * j + y) for z, y in order] for i in range(4) for j in range(4)]


def pair_pairs():
    return [
        (at(0, 2 * m + i, 2 * m + j), at(0, 2 * m + i, 2 * m + 1 - j))
        for m in range(4)
        for i in range(2)
        for j in range(2)
    ]


def hop_pairs(step):
    return [
        (at(step, 2 * m + i, 2 * m + j), at(step + 1, 2 * m + i, 2 * m + j))
        for m in range(4)
        for i in range(2)
        for j in range(2)
    ]


def position():
    section, blk, head = lax.axis_index("section"), lax.axis_index("blk"), lax.axis_index("head")
    z_low = lax.rem(blk // 4, 2)
    odd = lax.rem(section, 2)
    half = jnp.where(odd == 1, z_low, head)
    side = jnp.where(odd == 1, head, z_low)
    return section, odd, blk // 8, half, side


def head_norm(block, gain):
    mean = jnp.mean(block * block, axis=-1, keepdims=True)
    return block * lax.rsqrt(mean + 1e-06) * gain


def pack_kernel(w_ref, stale_ref, hidden_ref, out_ref):
    micros, width = hidden_ref.shape[0], out_ref.shape[2]
    sides = [slice(0, width), slice(width, 2 * width)]
    for m in range(micros):
        states = [hidden_ref[m, :, cols].astype(F32) for cols in sides]
        states = jnp.concatenate(states, axis=0).astype(BF)
        for side, cols in enumerate(sides):
            place = 2 * micros - 1 - (2 * m + side)
            for part in range(3):
                out_ref[place, part * ROWS : (part + 1) * ROWS, :] = w_ref[part, :, cols]
            old = [stale_ref[part, m, :, cols].astype(F32) for part in range(2)]
            old = jnp.concatenate(old, axis=0).astype(BF)
            out_ref[place, 3 * ROWS : 3 * ROWS + 16, :] = old
            out_ref[place, 3 * ROWS + 16 : PIECE, :] = states


def with_blocks(pieces, act):
    _, odd, micro, half, _ = position()
    evens, odds = [], []
    for ahead in range(4):
        far = lax.rem(micro + ahead, 4)
        for lane in range(2):
            local = 7 + lane
            even_piece = pieces[MOVES.index((ahead, lane)) if ahead else local]
            odd_piece = pieces[MOVES.index((ahead, lane)) if ahead or lane else local]
            z = 2 * far + (half if lane == 0 else 1 - half)
            for j in range(4):
                evens.append((even_piece.at[j], (7 - 4 * lane - j) * 4 + far))
                odds.append((odd_piece.at[j], z * 4 + 3 - j))
    for parity, blocks in enumerate((evens, odds)):

        @pl.when(odd == parity)
        def _(blocks=blocks):
            for i, (source, block) in enumerate(blocks):
                act(i, source, block)


def tail_kernel(heads, *refs):
    flag_ref, patch_ref, text_len_ref, qk_ref = refs[:4]
    pieces, (info_ref, sk_ref, sv_ref, state_ref) = refs[4:13], refs[13:17]
    tails, stale_key, stale_value, state, sems = refs[17:]
    section, _, micro, _, _ = position()

    def tail_copy(i, source, block):
        return pltpu.make_async_copy(
            source.at[pl.ds(3 * ROWS, TAIL), :], tails.at[block], sems.at[i]
        )

    with_blocks(pieces, lambda *block: tail_copy(*block).start())
    line = lax.broadcasted_iota(jnp.int32, info_ref.shape, 0)
    limits = jnp.where(line == 1, patch_ref[micro], text_len_ref[0])
    info_ref[...] = jnp.where(line == 0, flag_ref[micro, section], limits)
    with_blocks(pieces, lambda *block: tail_copy(*block).wait())
    for b in range(32):
        tail = tails[b].astype(F32)
        stale_key[8 * b : 8 * b + 8, :] = tail[0:8]
        stale_value[8 * b : 8 * b + 8, :] = tail[8:16]
        state[0, 8 * b : 8 * b + 8, :] = tail[16:24]
        state[1, 8 * b : 8 * b + 8, :] = tail[24:32]
    sv_ref[...] = stale_value[...].astype(BF)
    state_ref[...] = state[...].astype(BF)
    for h in range(heads):
        cols = slice(h * 128, (h + 1) * 128)
        sk_ref[:, cols] = head_norm(stale_key[:, cols], qk_ref[1:2, :]).astype(BF)


def prep_kernel(heads, *refs):
    text_ref, gain_ref, qk_ref = refs[:3]
    pieces, (w_ref, tk_ref, tv_ref), (held, sems) = refs[3:12], refs[12:15], refs[15:]
    width = heads * 128

    def weight_copies(i, source, block):
        row = pl.multiple_of(block * ROWS, 16)
        return [
            pltpu.make_async_copy(
                source.at[pl.ds(part * ROWS, ROWS), :],
                held.at[pl.ds(row, ROWS), pl.ds(part * width, width)],
                sems.at[3 * i + part],
            )
            for part in range(3)
        ]

    with_blocks(pieces, lambda *block: [copy.start() for copy in weight_copies(*block)])
    text = text_ref[...].astype(F32)
    mean = jnp.mean(text * text, axis=-1, keepdims=True)
    normed = (text * lax.rsqrt(mean + 1e-06) * gain_ref[...]).astype(BF)
    with_blocks(pieces, lambda *block: [copy.wait() for copy in weight_copies(*block)])
    store = pltpu.make_async_copy(held, w_ref, sems.at[96])
    store.start()
    kv = jnp.dot(normed, held[:, width:], preferred_element_type=F32).astype(BF)
    for h in range(heads):
        cols = slice(h * 128, (h + 1) * 128)
        tk_ref[:, cols] = head_norm(kv[:, cols].astype(F32), qk_ref[1:2, :]).astype(BF)
    tv_ref[...] = kv[:, width:]
    store.wait()


def layer_kernel(
    heads, info_ref, x_ref, w_ref, gain_ref, qk_ref, tk_ref, tv_ref,
    sk_ref, sv_ref, out_ref, cache_ref,
):
    width = heads * 128
    _, _, _, half, side = position()
    stale, limit, text_limit = info_ref[0:1, :] == 1, info_ref[1:2, 0:1], info_ref[2:3, 0:1]
    own_ref = x_ref.at[2 * half + side]
    parts = [x_ref[q].astype(F32) for q in range(4)]
    total = sum(jnp.sum(part * part, axis=-1, keepdims=True) for part in parts)
    scale = lax.rsqrt(total / (4 * width) + 1e-06)
    normed = jnp.concatenate(
        [
            (part * scale * gain_ref[:, q * width : (q + 1) * width]).astype(BF)
            for q, part in enumerate(parts)
        ],
        axis=1,
    )
    projected = jnp.dot(normed, w_ref[...], preferred_element_type=F32)
    fresh = projected[:, width:].astype(BF)
    cache_ref[0] = fresh[:, :width]
    cache_ref[1] = fresh[:, width:]
    query_gain, key_gain = qk_ref[0:1, :], qk_ref[1:2, :]
    tokens = out_ref.shape[0]
    own_mask = lax.broadcasted_iota(jnp.int32, (tokens, tokens), 1) < limit
    text_mask = lax.broadcasted_iota(jnp.int32, (tokens, tk_ref.shape[0]), 1) < text_limit
    contract = (((1,), (1,)), ((), ()))
    for h in range(heads):
        cols = slice(h * 128, (h + 1) * 128)
        queries = head_norm(projected[:, cols], query_gain).astype(BF)
        keys = head_norm(fresh[:, cols].astype(F32), key_gain).astype(BF)
        keys = jnp.where(stale, sk_ref[:, cols], keys)
        values = jnp.where(stale, sv_ref[:, cols], fresh[:, width + h * 128 : width + (h + 1) * 128])
        own = lax.dot_general(queries, keys, contract, preferred_element_type=F32)
        own = jnp.where(own_mask, jnp.exp(own * 128 ** (-0.5)), 0.0)
        text = lax.dot_general(queries, tk_ref[:, cols], contract, preferred_element_type=F32)
        text = jnp.where(text_mask, jnp.exp(text * 128 ** (-0.5)), 0.0)
        numerator = jnp.dot(text.astype(BF), tv_ref[:, cols], preferred_element_type=F32)
        numerator += jnp.dot(own.astype(BF), values, preferred_element_type=F32)
        denominator = jnp.sum(own, axis=1, keepdims=True) + jnp.sum(text, axis=1, keepdims=True)
        out_ref[:, cols] = (own_ref[:, cols].astype(F32) + numerator / denominator).astype(BF)


def shards(
    hidden_in, w_qkv, norm_gain, qk_gain, text_states, text_len, patch_len, stale_flags, stale_kv
):
    sections = lax.axis_size("section")
    section = lax.axis_index("section")
    z = lax.axis_index("blk") // 4
    head = lax.axis_index("head")
    odd = section % 2 == 1
    micros, tok, half_width = hidden_in.shape
    width = half_width // 2
    heads = width // 128
    tokens, text_count, depth = 32 * tok, text_states.shape[1], text_states.shape[2]

    sources = [
        pltpu.with_memory_space_constraint(source, pltpu.HBM)
        for source in (jnp.moveaxis(w_qkv[0], 1, 0), stale_kv[0], hidden_in)
    ]
    packed = pl.pallas_call(
        pack_kernel,
        out_shape=jax.ShapeDtypeStruct((2 * micros, PIECE, width), BF),
        in_specs=[VMEM] * 3,
        out_specs=VMEM,
        compiler_params=pltpu.CompilerParams(vmem_limit_bytes=16 * 2**20),
        name="pack",
    )(*sources)
    ring = lax.all_to_all(packed, AX, 0, 0, axis_index_groups=ring_groups(sections), tiled=True)
    by_half = ring.reshape(4, 2, PIECE, width)
    low = z % 2 == 1
    lanes = (
        jnp.where(odd, jnp.where(low, by_half[:, 0], by_half[:, 1]), ring[:4]),
        jnp.where(odd, jnp.where(low, by_half[:, 1], by_half[:, 0]), ring[4:]),
    )
    pieces = [lax.ppermute(lanes[lane], AX, move_pairs(ahead, lane, sections)) for ahead, lane in MOVES]
    pieces = [
        *[pltpu.with_memory_space_constraint(piece, pltpu.HBM) for piece in pieces[:-2]],
        *pieces[-2:],
        *[pltpu.with_memory_space_constraint(lane, pltpu.HBM) for lane in lanes],
    ]

    qk = qk_gain[0]
    block = jax.ShapeDtypeStruct((tokens, width), BF)
    text_block = jax.ShapeDtypeStruct((text_count, width), BF)
    info, stale_key, stale_value, state = pl.pallas_call(
        functools.partial(tail_kernel, heads),
        out_shape=[
            jax.ShapeDtypeStruct((8, 128), jnp.int32),
            block,
            block,
            jax.ShapeDtypeStruct((2, tokens, width), BF),
        ],
        in_specs=[SMEM] * 3 + [VMEM] + [HBM] * 9,
        out_specs=[VMEM] * 4,
        scratch_shapes=[
            pltpu.VMEM((32, TAIL, width), BF),
            pltpu.VMEM((tokens, width), F32),
            pltpu.VMEM((tokens, width), F32),
            pltpu.VMEM((2, tokens, width), F32),
            pltpu.SemaphoreType.DMA((32,)),
        ],
        compiler_params=pltpu.CompilerParams(vmem_limit_bytes=16 * 2**20),
        name="tails",
    )(stale_flags, patch_len, text_len, qk, *pieces)
    other = lax.ppermute(state, AX, pair_pairs())
    weights, text_key, text_value = pl.pallas_call(
        functools.partial(prep_kernel, heads),
        out_shape=[jax.ShapeDtypeStruct((depth, 3 * width), BF), text_block, text_block],
        in_specs=[VMEM] * 3 + [HBM] * 9,
        out_specs=[HBM] + [VMEM] * 2,
        scratch_shapes=[pltpu.VMEM((depth, 3 * width), BF), pltpu.SemaphoreType.DMA((97,))],
        compiler_params=pltpu.CompilerParams(vmem_limit_bytes=16 * 2**20),
        cost_estimate=pl.CostEstimate(
            flops=4 * text_count * depth * width,
            bytes_accessed=12 * depth * width,
            transcendentals=0,
        ),
        name="prepare",
    )(text_states[0], norm_gain, qk, *pieces)
    whole = jnp.where(
        head == 0, jnp.concatenate([state, other]), jnp.concatenate([other, state])
    )

    layer = pl.pallas_call(
        functools.partial(layer_kernel, heads),
        out_shape=[block, jax.ShapeDtypeStruct((2, tokens, width), BF)],
        in_specs=[VMEM] * 9,
        out_specs=[VMEM] * 2,
        compiler_params=pltpu.CompilerParams(vmem_limit_bytes=16 * 2**20),
        name="layer",
    )

    weights = pltpu.with_memory_space_constraint(weights, pltpu.HBM)
    rest = (weights, norm_gain, qk, text_key, text_value, stale_key, stale_value)

    def advance(step, entering):
        whole = lax.all_to_all(
            jnp.broadcast_to(entering[None], (4,) + entering.shape),
            PLANE, 0, 0, axis_index_groups=block_groups(step % 2 == 0), tiled=True,
        )
        return tuple(layer(info, whole, *rest))

    kept = (jnp.zeros((tokens, width), BF), jnp.zeros((2, tokens, width), BF))
    kept = lax.cond(
        section == 0, lambda whole, *kept: tuple(layer(info, whole, *rest)), lambda whole, *kept: kept,
        whole, *kept,
    )
    for step in range(1, sections):
        entering = lax.ppermute(kept[0], AX, hop_pairs(step - 1))
        kept = lax.cond(
            section == step,
            lambda entering, *kept: advance(step, entering),
            lambda entering, *kept: kept,
            entering, *kept,
        )

    result = jnp.concatenate([kept[0][None], kept[1]]).reshape(3, 32, tok, width)
    result = lax.all_to_all(jnp.moveaxis(result, 1, 0), "blk", 0, 0, tiled=True)
    found = [
        jnp.stack([result[(2 * m + j) * 4 + m] for m in range(micros)]) for j in range(2)
    ]
    swap = [
        (at(s, 0, 0) + 2 * b + h, at(s, 0, 0) + 2 * b + 1 - h)
        for s in range(1, sections, 2)
        for b in range(32)
        for h in range(2)
    ]
    other = lax.ppermute(jnp.where(head == 0, found[1], found[0]), AX, swap)
    left = jnp.where(odd & (head == 1), other, found[0])
    right = jnp.where(odd & (head == 0), other, found[1])
    sides = jnp.stack([left, right])
    hidden = sides[:, :, 0].transpose(1, 2, 0, 3).reshape(1, micros, tok, half_width)
    cache = sides[:, :, 1:].transpose(2, 1, 3, 0, 4).reshape(1, 2, micros, tok, half_width)
    return (hidden, cache)


def solution(mesh):
    in_specs = (
        P(None, "blk", "head"),
        P("section", "blk", None, "head"),
        P("section", None),
        P("section", None, None),
        P("section", None, None),
        P(),
        P(),
        P(),
        P("section", None, None, "blk", "head"),
    )
    out_specs = (P("section", None, "blk", "head"), P("section", None, None, "blk", "head"))
    return jax.shard_map(shards, mesh=mesh, in_specs=in_specs, out_specs=out_specs, check_vma=False)
```
